32 devices in a mesh: dp: 1, ctx: 32 (over z, y, x, core), tp: 1.
Axes of the slice: x: 2, y: 2, z: 4, core: 2. Of those that a mesh axis runs over, the one named last changes fastest.
Arguments:
- queries: bfloat16 [1, 8192, 2048], P('dp', 'ctx', 'tp'), may hold values from -6 to 6
- key_rows: bfloat16 [1, 8192, 2048], P('dp', 'ctx', 'tp'), may hold values from -0.5390625 to 0.5390625
- value_rows: bfloat16 [1, 8192, 2048], P('dp', 'ctx', 'tp'), may hold values from -6 to 6
- out_grad: bfloat16 [1, 8192, 2048], P('dp', 'ctx', 'tp'), may hold values from -24 to 24
- norm_gain: float32 [16, 128], P('tp'), may hold values from 0.1 to 1.9
- doc_ids: int32 [1, 64], P('dp', 'ctx'), may hold values from 0 to 3, never falling along the last dimension, each value on 1 to 32 neighbouring positions
Outputs:
- query_grad: bfloat16 [1, 8192, 2048], P('dp', 'ctx', 'tp')
- key_grad: bfloat16 [1, 8192, 2048], P('dp', 'ctx', 'tp')
- value_grad: bfloat16 [1, 8192, 2048], P('dp', 'ctx', 'tp')
- gain_grad: float32 [16, 128], P('tp', 'dp')
The draws below stay inside these ranges and needn't reach their ends.
Inputs may be any that keep to these rules, and one draw needn't show every extreme that they name: `doc_ids`: ids never fall along a sequence; each id covers at most 32 consecutive blocks.
All inputs are finite; a program needn't handle non-finite values.
Results may differ from the reference program's by a relative error of at most 0.0062.
Values sent between devices are 32-bit elements; how exact they have to be, the bound alone decides.
No kernel may reach another device: no remote copies, remote signals or barrier semaphores. Data moves between devices by JAX's collectives and lax.ppermute only.
A program may use at most 128 MiB of HBM per device.

```python
import math
import jax
import jax.numpy as jnp
import numpy as np
from jax import lax

HEADS = 16
DH = 128
STRETCH = 256
BLK = 128
LEN = 8192
SEQS = 1
NBLK = 64
NDOCS = 4
DOC_MOST = 32


def draw_out_grad(key, part):
    key = jax.random.fold_in(key, 7)
    first_key = jax.random.fold_in(key, 0)
    full_shape = (SEQS, LEN, HEADS * DH)
    ramp = 1.0 + 2.0 * jnp.arange(LEN, dtype=jnp.float32) / (LEN - 1)
    values = jax.random.normal(first_key, full_shape, jnp.float32) * ramp[None, :, None]
    return jnp.clip(values, -24.0, 24.0).astype(jnp.bfloat16)


def levels(stream_key, dims, shards, low, largest):
    def one(axis_at, blocks):
        heights = jax.random.uniform(jax.random.fold_in(jax.random.fold_in(stream_key, 6), axis_at), (blocks,), jnp.float32, low / len(shards), largest / len(shards))
        return jnp.repeat(jnp.exp(heights), dims[axis_at] // blocks).reshape((-1,) + (1,) * (len(dims) - axis_at - 1))

    factor_of = one(*shards[0])
    for cut in shards[1:]:
        factor_of = factor_of * one(*cut)
    return factor_of


def profile(amount, total, reach, slope):
    weights = [(1 << 20) // math.isqrt(standing ** slope) + 1 for standing in range(2, amount + 1)]
    spare, holding = total - reach - (amount - 1), [1] * (amount - 1)
    while spare > 0:
        free = [i for i in range(amount - 1) if holding[i] < reach]
        whole, left = sum([weights[i] for i in free]), spare
        for i in free:
            extra = min(reach - holding[i], max(1, left * weights[i] // whole), spare)
            holding[i] = holding[i] + extra
            spare = spare - extra
    return np.array([reach] + holding)


def ragged_sizes(own_key, count, total, limit, slope):
    if count == 2:
        one = jax.random.randint(own_key, (), max(1, total - limit), min(limit, total - 1) + 1)
        return jnp.stack([one, total - one])
    tallies = jnp.asarray(profile(count, total, limit, slope), jnp.int32)
    pairs = (count - 1) // 2
    source_of, sink = tallies[1:1 + 2 * pairs:2], tallies[2:2 + 2 * pairs:2]
    margin = jnp.minimum(source_of - 1, limit - sink)
    moved = jax.random.randint(jax.random.fold_in(own_key, 1), (pairs,), 0, 1 << 20) % (margin + 1)
    tallies = tallies.at[1:1 + 2 * pairs:2].set(source_of - moved).at[2:2 + 2 * pairs:2].set(sink + moved)
    return tallies[jax.random.permutation(jax.random.fold_in(own_key, 2), count)]


def noise(stream_key, shape, deviation, bound, cuts=(), kind=jnp.bfloat16):
    entries = deviation * jax.random.normal(stream_key, shape, jnp.float32)
    if cuts:
        entries = entries * levels(stream_key, shape, cuts, -0.22, 0.18)
    return jnp.clip(entries, -bound, bound).astype(kind)


def setup_inputs(seed: int = 0) -> dict:
    key_list = jax.random.split(jax.random.key(seed), 7)
    return {
        "queries": noise(key_list[0], (SEQS, LEN, HEADS * DH), 1.0, 6.0, ((1, 32),)),
        "key_rows": noise(key_list[1], (SEQS, LEN, HEADS * DH), 0.09, 0.5390625, ((1, 32),)),
        "value_rows": noise(key_list[2], (SEQS, LEN, HEADS * DH), 1.0, 6.0, ((1, 32),)),
        "out_grad": draw_out_grad(jax.random.fold_in(key_list[6], 71), 0),
        "norm_gain": jnp.clip(1.0 + 0.18 * jax.random.normal(key_list[4], (HEADS, DH), jnp.float32), 0.1, 1.9),
        "doc_ids": jax.vmap(lambda own: jnp.searchsorted(jnp.cumsum(ragged_sizes(own, NDOCS, NBLK, DOC_MOST, 1)), jnp.arange(NBLK), side="right"))(jax.random.split(key_list[5], SEQS)).reshape((SEQS, NBLK)).astype(jnp.int32),
    }


EPSILON = 1e-06
EXACT = lax.Precision.HIGHEST

def causal_mask(docs):
    length = docs.shape[0]
    positions = jnp.arange(length)
    return (positions[:, None] >= positions[None, :]) & (docs[:, None] == docs[None, :])

def merge_pair(former, latter):
    matches = (latter[1] == former[1]).astype(former[0].dtype)
    return (latter[0] + matches * former[0], latter[1])

def rounded(values):
    return lax.optimization_barrier(values.astype(jnp.bfloat16)).astype(jnp.float32)

def one_sequence(queries, key_rows, value_rows, out_grad, doc_row, norm_gain):
    stretches = LEN // STRETCH
    stretch_shape = (stretches, STRETCH, HEADS, DH)
    query_full = queries.reshape(stretch_shape).astype(jnp.float32)
    key_full = key_rows.reshape(stretch_shape).astype(jnp.float32)
    value_full = value_rows.reshape(stretch_shape).astype(jnp.float32)
    grad_full = out_grad.reshape(stretch_shape).astype(jnp.float32)
    docs = jnp.repeat(doc_row, BLK).astype(jnp.float32).reshape(stretches, STRETCH)
    gain_full = norm_gain.astype(jnp.float32)
    start = (jnp.zeros((HEADS, DH, DH), jnp.float32), jnp.float32(-1.0))

    def forward(carried, pieces):
        query_c, key_c, value_c, grad_c, doc_c = pieces
        state, prior_id = carried
        state_round = rounded(state)
        enter_weight = (doc_c == prior_id).astype(jnp.float32)
        inter = jnp.einsum('thd,hde->the', query_c * enter_weight[:, None, None], state_round, precision=EXACT)
        scores = jnp.einsum('thd,shd->hts', query_c, key_c, precision=EXACT)
        scores = rounded(jnp.where(causal_mask(doc_c)[None], scores, 0.0))
        attended = inter + jnp.einsum('hts,she->the', scores, value_c, precision=EXACT)
        inv_rms = lax.rsqrt(lax.optimization_barrier(jnp.mean(attended * attended, -1, keepdims=True)) + EPSILON)
        scaled = grad_c * gain_full
        gain_term = lax.optimization_barrier(jnp.sum(grad_c * attended * inv_rms, 0))
        attn_grad = inv_rms * scaled - inv_rms ** 3 * attended * lax.optimization_barrier(jnp.mean(scaled * attended, -1, keepdims=True))
        attn_grad = attn_grad.astype(jnp.bfloat16)
        last_id = doc_c[-1]
        last_weight = (doc_c == last_id).astype(jnp.float32)
        element = jnp.einsum('shd,she->hde', key_c * last_weight[:, None, None], value_c, precision=EXACT)
        return (merge_pair(carried, (element, last_id)), (attn_grad, state_round, prior_id, gain_term))
    ignored, saved = lax.scan(forward, start, (query_full, key_full, value_full, grad_full, docs))
    attn_grads, states_in, ids_in, gain_terms = saved

    def backward(carried, pieces):
        query_c, key_c, value_c, doc_c, attn_c, state, prior_id = pieces
        grad_state, next_id = carried
        grad_round = rounded(grad_state)
        attn_full = attn_c.astype(jnp.float32)
        enter_weight = (doc_c == prior_id).astype(jnp.float32)
        leave_weight = (doc_c == next_id).astype(jnp.float32)
        mask = causal_mask(doc_c)[None]
        scores = rounded(jnp.where(mask, jnp.einsum('thd,shd->hts', query_c, key_c, precision=EXACT), 0.0))
        pair_grad = rounded(jnp.where(mask, jnp.einsum('the,she->hts', attn_full, value_c, precision=EXACT), 0.0))
        query_grad = jnp.einsum('the,hde->thd', attn_full * enter_weight[:, None, None], state, precision=EXACT)
        query_grad = query_grad + jnp.einsum('hts,shd->thd', pair_grad, key_c, precision=EXACT)
        key_grad = jnp.einsum('hts,thd->shd', pair_grad, query_c, precision=EXACT)
        key_grad = key_grad + jnp.einsum('she,hde->shd', value_c * leave_weight[:, None, None], grad_round, precision=EXACT)
        value_grad = jnp.einsum('hts,the->she', scores, attn_full, precision=EXACT)
        value_grad = value_grad + jnp.einsum('shd,hde->she', key_c * leave_weight[:, None, None], grad_round, precision=EXACT)
        first_id = doc_c[0]
        first_weight = (doc_c == first_id).astype(jnp.float32)
        element = jnp.einsum('thd,the->hde', query_c * first_weight[:, None, None], attn_full, precision=EXACT)
        outputs = (query_grad.astype(jnp.bfloat16), key_grad.astype(jnp.bfloat16), value_grad.astype(jnp.bfloat16))
        return (merge_pair(carried, (element, first_id)), outputs)
    ignored, grads = lax.scan(backward, start, (query_full, key_full, value_full, docs, attn_grads, states_in, ids_in), reverse=True)
    query_grad, key_grad, value_grad = grads
    flat_shape = (LEN, HEADS * DH)
    return (query_grad.reshape(flat_shape), key_grad.reshape(flat_shape), value_grad.reshape(flat_shape), lax.optimization_barrier(jnp.sum(gain_terms, 0)))

def reference(queries, key_rows, value_rows, out_grad, norm_gain, doc_ids):

    def per_sequence(pieces):
        return one_sequence(pieces[0], pieces[1], pieces[2], pieces[3], pieces[4], norm_gain)
    query_grad, key_grad, value_grad, gain_parts = lax.map(per_sequence, (queries, key_rows, value_rows, out_grad, doc_ids))
    return (query_grad, key_grad, value_grad, lax.optimization_barrier(jnp.sum(gain_parts, 0)))
```

```python
import functools

import jax
import jax.numpy as jnp
from jax import lax
from jax.experimental import pallas as pl
from jax.experimental.pallas import tpu as pltpu
from jax.sharding import PartitionSpec as P

BLK = 128
EPSILON = 1e-06
CHIPS = 4
GROUP = 2 * CHIPS
IDS = 8
FIRST, LAST = 0, 1
F32, BF16 = jnp.float32, jnp.bfloat16


def dot(left, right, left_dim, right_dim):
    return lax.dot_general(
        left, right, (((left_dim,), (right_dim,)), ((), ())), preferred_element_type=F32
    )


def my_core():
    return lax.axis_index("ctx") % 2


def my_chip():
    return (lax.axis_index("ctx") // 2) % CHIPS


def turned(turn):
    return (0, 1 + my_core(), 2 - my_core(), 3)[turn]


def one_doc(docs):
    return jnp.where(docs[0, 0] == docs[0, 1], 1.0, 0.0)


def column(docs, first_block, dtype):
    rows = lax.broadcasted_iota(jnp.int32, (2 * BLK, 1), 0)
    own = (rows < BLK) if first_block else (rows >= BLK)
    return jnp.where(own, 1.0, one_doc(docs)).astype(dtype)


def lower(table, both):
    rows = lax.broadcasted_iota(jnp.int32, (BLK, BLK), 0)
    cols = lax.broadcasted_iota(jnp.int32, (BLK, BLK), 1)
    keep = rows >= cols
    upper = jnp.where(keep, table[:BLK, :BLK], 0.0).astype(BF16)
    below = (table[BLK:, :BLK] * both).astype(BF16)
    right = jnp.where(keep, table[BLK:, BLK:], 0.0).astype(BF16)
    return upper, jnp.concatenate([below, right], 1)


def higher(table, both):
    rows = lax.broadcasted_iota(jnp.int32, (BLK, BLK), 0)
    cols = lax.broadcasted_iota(jnp.int32, (BLK, BLK), 1)
    keep = rows <= cols
    left = jnp.where(keep, table[:BLK, :BLK], 0.0).astype(BF16)
    above = (table[:BLK, BLK:] * both).astype(BF16)
    below = jnp.where(keep, table[BLK:, BLK:], 0.0).astype(BF16)
    return jnp.concatenate([left, above], 1), below


def times_lower(masked, values):
    upper, below = masked
    return jnp.concatenate([dot(upper, values[:BLK], 1, 0), dot(below, values, 1, 0)], 0)


def times_higher(masked, values):
    above, lower_right = masked
    return jnp.concatenate([dot(above, values, 1, 0), dot(lower_right, values[BLK:], 1, 0)], 0)


def write_ids(docs, out, rows, backward):
    first, last = docs[0, 0].astype(F32), docs[0, 1].astype(F32)
    if backward:
        first, last = -last, -first
    out[pl.ds(rows, IDS), :] = jnp.zeros((IDS, 128), F32)
    out[pl.ds(rows + FIRST, 1), :] = jnp.full((1, 128), first, F32)
    out[pl.ds(rows + LAST, 1), :] = jnp.full((1, 128), last, F32)


def wide(base, head):
    return pl.ds(pl.multiple_of((base + head) * 128, 128), 128)


def element_kernel(docs, key, value, out, *, half, other):
    base = (1 - my_core() if other else my_core()) * half
    weight = column(docs, False, BF16)
    write_ids(docs, out, half * 128, False)
    for head in range(half):
        at = wide(base, head)
        out[pl.ds(head * 128, 128), :] = dot(key[:, at] * weight, value[:, at], 0, 0)


def intra_kernel(docs, query, key, value, grad, own, message, *, half):
    both = one_doc(docs)
    tokens = query.shape[0]
    for other in (True, False):
        base = (1 - my_core() if other else my_core()) * half
        for head in range(half):
            full, cols = wide(base, head), pl.ds(head * 128, 128)
            q = query[:, full]
            scores = lower(dot(q, key[:, full], 1, 1), both)
            part = times_lower(scores, value[:, full])
            if other:
                message[pl.ds(0, tokens), cols] = q.astype(F32)
                message[pl.ds(tokens, tokens), cols] = grad[:, full].astype(F32)
                message[pl.ds(2 * tokens, tokens), cols] = part
            else:
                own[:, cols] = part


def attend(q, g, intra, state, gain, joined):
    inter = dot(q, state, 1, 0)
    attended = intra + jnp.concatenate([inter[:BLK], inter[BLK:] * joined], 0)
    inv_rms = lax.rsqrt(jnp.mean(attended * attended, -1, keepdims=True) + EPSILON)
    scaled = g * gain
    normed = attended * inv_rms
    terms = jnp.sum(g * normed, 0, keepdims=True)
    mean = jnp.mean(scaled * normed, -1, keepdims=True)
    attn = (inv_rms * (scaled - normed * mean)).astype(BF16)
    back = dot(q[:BLK], attn[:BLK], 0, 0) + dot(q[BLK:], attn[BLK:], 0, 0) * joined
    return attn, back, terms


def middle_kernel(
    docs, own, other, c0, c1, c2, c3, query, grad, intra, message, gain,
    up0, up1, up2, up3, back_own, back_other, attn_own, reply, state_own, *, half, size,
):
    rows, tokens, chunk = half * 128, query.shape[0], size // 128
    base = my_core() * half
    is_first = my_core() == 0
    own_first, own_last = row(own, rows, FIRST), row(own, rows, LAST)
    other_first, other_last = row(other, rows, FIRST), row(other, rows, LAST)
    keep_coming, keep_other, send_coming, send_own = spread_weights(
        is_first, own_first, own_last, other_first, other_last
    )
    own_joined, other_joined = match(own_first, own_last), match(other_first, other_last)
    for back, first, last in ((back_own, own_first, own_last), (back_other, other_first, other_last)):
        back[pl.ds(rows, IDS), :] = jnp.zeros((IDS, 128), F32)
        back[pl.ds(rows + FIRST, 1), :] = -last
        back[pl.ds(rows + LAST, 1), :] = -first
    first = jnp.minimum(own_first, other_first)
    last = jnp.maximum(own_last, other_last)
    own_weight, other_weight = match(own_first, first), match(other_first, first)
    ups = (up0, up1, up2, up3)
    for up in ups:
        up[pl.ds(size, 2 * IDS), :] = jnp.zeros((2 * IDS, 128), F32)
        up[pl.ds(size + FIRST, 1), :] = -last
        up[pl.ds(size + LAST, 1), :] = -first
    for turn, chip in enumerate((c0, c1, c2, c3)):
        for step in range(chunk):
            head = lax.bitwise_xor(my_chip(), turned(turn)) * chunk + step
            cols, full = wide(0, head), wide(base, head)
            coming = chip[pl.ds(step * 128, 128), :]
            state = (coming * keep_coming + other[cols, :] * keep_other).astype(BF16)
            state_own[cols, :] = state
            state_other = coming * send_coming + own[cols, :] * send_own
            reply[pl.ds(tokens, 128), cols] = state_other
            weights = gain[pl.ds(base + head, 1), :]
            attn, back, terms = attend(
                query[:, full], grad[:, full].astype(F32), intra[:, cols], state, weights, own_joined
            )
            attn_own[:, cols] = attn
            back_own[cols, :] = back
            attn, back_far, terms_far = attend(
                message[pl.ds(0, tokens), cols].astype(BF16),
                message[pl.ds(tokens, tokens), cols],
                message[pl.ds(2 * tokens, tokens), cols],
                state_other.astype(BF16),
                weights,
                other_joined,
            )
            reply[pl.ds(0, tokens), cols] = attn.astype(F32)
            back_other[cols, :] = back_far
            ups[turn][pl.ds(step * 128, 128), :] = back * own_weight + back_far * other_weight
            for up in ups:
                up[pl.ds(size + IDS + head, 1), :] = terms + terms_far


def within_kernel(docs, query, key, value, *refs, half, other):
    query_grad, key_part, value_part, held, sems = refs[-5:]
    tokens = query.shape[0]
    both = one_doc(docs)
    enter32 = column(docs, True, F32)
    base = (1 - my_core() if other else my_core()) * half
    copies = []
    for head in range(half):
        cols = pl.ds(head * 128, 128)
        full = wide(base, head)
        q, k, v = query[:, full], key[:, full], value[:, full]
        if other:
            a = refs[0][pl.ds(0, tokens), cols].astype(BF16)
            state = refs[0][pl.ds(tokens, 128), cols].astype(BF16)
        else:
            a, state = refs[0][:, cols], refs[1][cols, :]
        pair = lower(dot(a, v, 1, 1), both)
        cross = enter32 * dot(a, state, 1, 1)
        held[:, cols] = (cross + times_lower(pair, k)).astype(BF16)
        key_part[:, cols] = times_higher(higher(dot(v, a, 1, 1), both), q)
        value_part[:, cols] = times_higher(higher(dot(k, q, 1, 1), both), a)
        copies.append(pltpu.make_async_copy(held.at[:, cols], query_grad.at[:, full], sems.at[head]))
        copies[-1].start()
    for copy in copies:
        copy.wait()


def finish_kernel(docs, key, value, key_part, value_part, state, *refs, half, other):
    refs, (key_held, value_held, sems) = refs[:-3], refs[-3:]
    if other:
        refs, gain_grad = refs[:-1], refs[-1]
        for head in range(half):
            gain_grad[pl.ds(my_core() * half + head, 1), :] = refs[0][pl.ds(head, 1), :]
            gain_grad[pl.ds((1 - my_core()) * half + head, 1), :] = state[pl.ds(half * 128 + head, 1), :]
    key_grad, value_grad = refs[-2:]
    leave = column(docs, False, F32)
    base = (1 - my_core() if other else my_core()) * half
    copies = []
    for head in range(half):
        cols = pl.ds(head * 128, 128)
        full = wide(base, head)
        g = state[cols, :].astype(BF16)
        key_held[:, cols] = (key_part[:, cols] + leave * dot(value[:, full], g, 1, 1)).astype(BF16)
        value_held[:, cols] = (value_part[:, cols] + leave * dot(key[:, full], g, 1, 0)).astype(BF16)
        copies.append(pltpu.make_async_copy(key_held.at[:, cols], key_grad.at[:, full], sems.at[0, head]))
        copies.append(pltpu.make_async_copy(value_held.at[:, cols], value_grad.at[:, full], sems.at[1, head]))
        copies[-2].start()
        copies[-1].start()
    for copy in copies:
        copy.wait()


def row(ref, rows, which):
    return ref[pl.ds(rows + which, 1), :]


def match(left, right):
    return jnp.where(left == right, 1.0, 0.0)


def pair_kernel(docs, own, other, *outs, half, size):
    rows = half * 128
    first = jnp.minimum(row(own, rows, FIRST), row(other, rows, FIRST))
    last = jnp.maximum(row(own, rows, LAST), row(other, rows, LAST))
    own_weight = match(row(own, rows, LAST), last)
    other_weight = match(row(other, rows, LAST), last)
    for turn, out in enumerate(outs):
        owner = lax.bitwise_xor(my_chip(), turned(turn))
        part = pl.ds(pl.multiple_of(owner * size, size), size)
        out[pl.ds(0, size), :] = own[part, :] * own_weight + other[part, :] * other_weight
        out[pl.ds(size, IDS), :] = jnp.zeros((IDS, 128), F32)
        out[pl.ds(size + FIRST, 1), :] = first
        out[pl.ds(size + LAST, 1), :] = last


def plane_kernel(docs, c0, c1, c2, c3, out, *gain, size):
    chips = (c0, c1, c2, c3)
    last = functools.reduce(jnp.maximum, [row(c, size, LAST) for c in chips])
    out[pl.ds(0, size), :] = sum(
        c[pl.ds(0, size), :] * match(row(c, size, LAST), last) for c in chips
    )
    out[pl.ds(size, IDS), :] = jnp.zeros((IDS, 128), F32)
    out[pl.ds(size + LAST, 1), :] = last
    if gain:
        gain[0][...] = sum(c[pl.ds(size + IDS, IDS), :] for c in chips)
        out[pl.ds(size + IDS, IDS), :] = gain[0][...]


def chain_kernel(docs, c0, c1, c2, c3, *refs, size, distances, planes):
    chips = (c0, c1, c2, c3)
    backward = distances[0] < 0
    others, outs = refs[: len(distances)], refs[-CHIPS:]
    place = [lax.bitwise_xor(my_chip(), turned(turn)) for turn in range(CHIPS)]
    my_plane = lax.axis_index("ctx") // GROUP
    first = functools.reduce(jnp.minimum, [row(c, size, FIRST) for c in chips])
    coming = jnp.zeros((size, 128), F32)
    for distance, other in zip(distances, others):
        source = my_plane - distance
        inside = (source >= 0) & (source < planes)
        weight = match(row(other, size, LAST), first) * jnp.where(inside, 1.0, 0.0)
        coming = coming + other[pl.ds(0, size), :] * weight
    if backward:
        gain, sums, outs = refs[len(distances)], refs[-1], refs[-1 - CHIPS : -1]
        sums[...] = gain[...] + sum(p[pl.ds(size + IDS, IDS), :] for p in others)
    for turn, out in enumerate(outs):
        mine = row(chips[turn], size, FIRST)
        total = coming * match(mine, first)
        for other in range(CHIPS):
            if other == turn:
                continue
            ahead = place[other] > place[turn] if backward else place[other] < place[turn]
            weight = match(row(chips[other], size, LAST), mine) * jnp.where(ahead, 1.0, 0.0)
            total = total + chips[other][pl.ds(0, size), :] * weight
        out[...] = total


def spread_weights(is_first, own_first, own_last, other_first, other_last):
    ones = jnp.ones((1, 128), F32)
    joins = match(own_first, other_first)
    return (
        jnp.where(is_first, ones, joins),
        jnp.where(is_first, 0.0 * ones, match(other_last, own_first)),
        jnp.where(is_first, joins, ones),
        jnp.where(is_first, match(own_last, other_first), 0.0 * ones),
    )


def spread_kernel(docs, own, other, c0, c1, c2, c3, sums, sums_near, send, keep, total, *, half, size):
    rows = half * 128
    keep_coming, keep_other, send_coming, send_own = spread_weights(
        my_core() == 1,
        row(own, rows, FIRST),
        row(own, rows, LAST),
        row(other, rows, FIRST),
        row(other, rows, LAST),
    )
    for turn, chip in enumerate((c0, c1, c2, c3)):
        owner = lax.bitwise_xor(my_chip(), turned(turn))
        part = pl.ds(pl.multiple_of(owner * size, size), size)
        coming = chip[pl.ds(0, size), :]
        send[part, :] = coming * send_coming + own[part, :] * send_own
        keep[part, :] = (coming * keep_coming + other[part, :] * keep_other).astype(BF16)
    total[...] = sums[...] + sums_near[...]
    send[pl.ds(rows, IDS), :] = total[...]


def shape(rows, cols, dtype):
    return jax.ShapeDtypeStruct((rows, cols), dtype)


def call(kernel, docs, args, outs, flops=0, in_specs=None, out_specs=None, aliases=None, scratch=()):
    whole = pl.BlockSpec(memory_space=pltpu.VMEM)
    in_specs = in_specs or [None] * len(args)
    out_specs = out_specs or [None] * len(outs)
    moved = sum(a.size * a.dtype.itemsize for a in list(args) + list(outs))
    return pl.pallas_call(
        kernel,
        out_shape=outs,
        grid_spec=pltpu.PrefetchScalarGridSpec(
            num_scalar_prefetch=1,
            grid=(1,),
            in_specs=[spec or whole for spec in in_specs],
            out_specs=[spec or whole for spec in out_specs],
            scratch_shapes=scratch,
        ),
        input_output_aliases=aliases or {},
        cost_estimate=pl.CostEstimate(flops=flops, bytes_accessed=moved, transcendentals=0),
        compiler_params=pltpu.CompilerParams(vmem_limit_bytes=32 * 1024 * 1024),
    )(docs, *args)


def tie(value, *after):
    return lax.optimization_barrier((value, after))[0]


def local(queries, key_rows, value_rows, out_grad, norm_gain, doc_ids, *, shards, dp):
    tokens = queries.shape[1]
    heads, width = norm_gain.shape
    half = heads // 2
    rows, cols = half * width, heads * width
    size = rows // CHIPS
    query, key, value, grad = (
        a.reshape(tokens, cols) for a in (queries, key_rows, value_rows, out_grad)
    )
    planes = shards // GROUP
    any_place = pl.BlockSpec(memory_space=pl.ANY)

    def swap(value):
        return lax.ppermute(value, "ctx", [(i, i ^ 1) for i in range(shards)])

    def to_chips(values):
        return [values[0]] + [
            lax.ppermute(values[turn], "ctx", [(i, i ^ (2 * odd if i % 2 else 2 * even)) for i in range(shards)])
            for turn, even, odd in ((1, 1, 2), (2, 2, 1), (3, 3, 3))
        ]

    def around(value, distance):
        pairs = [(i, (i + distance * GROUP) % shards) for i in range(shards)]
        return lax.ppermute(value, "ctx", pairs)

    payload = shape(rows + IDS, width, F32)

    def chain(sent, backward, beside_up, beside_planes, beside_down):
        chunks = tie(to_chips(sent), beside_up(sent))
        plane, *gain = call(
            functools.partial(plane_kernel, size=size),
            doc_ids,
            chunks,
            [shape(size + (2 * IDS if backward else IDS), width, F32)]
            + ([shape(IDS, width, F32)] if backward else []),
        )
        distances = (-1, -2) if backward else (1, 2)
        others = [around(plane, distance) for distance in distances]
        others = tie(others, beside_planes(plane, others, *gain))
        sent = call(
            functools.partial(chain_kernel, size=size, distances=distances, planes=planes),
            doc_ids,
            [*chunks, *others, *gain],
            [shape(size, width, F32)] * CHIPS + ([shape(IDS, width, F32)] if backward else []),
        )
        return tie(to_chips(sent[:CHIPS]), beside_down(sent))

    def element(other):
        return call(
            functools.partial(element_kernel, half=half, other=other),
            doc_ids,
            [key, value],
            [payload],
            flops=2 * half * tokens * width * width,
        )[0]

    def within(other, sources, into):
        spare = [] if into is None else [into]
        at = 3 + len(sources)
        return call(
            functools.partial(within_kernel, half=half, other=other),
            doc_ids,
            [query, key, value, *sources, *spare],
            [shape(tokens, cols, BF16), shape(tokens, rows, F32), shape(tokens, rows, F32)],
            flops=2 * half * tokens * width * (6 * tokens + width),
            in_specs=[None] * at + [any_place] * len(spare),
            out_specs=[any_place] + [None] * 2,
            aliases={1 + at: 0} if spare else None,
            scratch=[pltpu.VMEM((tokens, rows), BF16), pltpu.SemaphoreType.DMA((half,))],
        )

    def finish(other, parts, state, sums, into):
        return call(
            functools.partial(finish_kernel, half=half, other=other),
            doc_ids,
            [key, value, *parts, state, *sums, *into],
            [shape(tokens, cols, BF16)] * 2 + [shape(heads, width, F32)] * len(sums),
            flops=2 * half * tokens * width * 2 * width,
            in_specs=[None] * (5 + len(sums)) + [any_place] * len(into),
            out_specs=[any_place] * 2 + [None] * len(sums),
            aliases={7: 0, 8: 1} if into else None,
            scratch=[
                pltpu.VMEM((tokens, rows), BF16),
                pltpu.VMEM((tokens, rows), BF16),
                pltpu.SemaphoreType.DMA((2, half)),
            ],
        )

    received = swap(element(True))
    own = element(False)
    sent = call(
        functools.partial(pair_kernel, half=half, size=size),
        doc_ids,
        [own, received],
        [shape(size + IDS, width, F32)] * CHIPS,
    )

    kept = {}

    def intra(sent):
        kept["inside"], kept["message"] = call(
            functools.partial(intra_kernel, half=half),
            doc_ids,
            [tie(query, sent), key, value, grad],
            [shape(tokens, rows, F32), shape(3 * tokens, rows, F32)],
            flops=2 * heads * tokens * width * 2 * tokens,
        )
        return kept["inside"]

    def forward_message(plane, others):
        kept["message"] = swap(tie(kept["message"], plane))
        return []

    coming = chain(sent, False, intra, forward_message, lambda sent: [])
    *sent, back, back_other, attn, reply, state = call(
        functools.partial(middle_kernel, half=half, size=size),
        doc_ids,
        [own, received, *coming, query, grad, kept["inside"], kept["message"], norm_gain],
        [shape(size + 2 * IDS, width, F32)] * CHIPS
        + [payload, payload]
        + [shape(tokens, rows, BF16), shape(tokens + width, rows, F32), shape(rows, width, BF16)],
        flops=2 * heads * tokens * width * 2 * width,
    )

    def beside_up(sent):
        kept["first"] = within(False, [tie(attn, sent), state], None)
        return kept["first"]

    def beside_planes(plane, others, gain):
        kept["reply"] = swap(tie(reply, plane))
        kept["near"] = around(tie(gain, others[1]), 1)
        return []

    def beside_down(sent):
        kept["sums"] = [sent[-1], kept["near"]]
        kept["second"] = within(True, [tie(kept["reply"], sent)], kept["first"][0])
        return kept["second"]

    coming = chain(sent, True, beside_up, beside_planes, beside_down)
    send, out_state, total = call(
        functools.partial(spread_kernel, half=half, size=size),
        doc_ids,
        [back, back_other, *coming, *kept["sums"]],
        [shape(rows + IDS, width, F32), shape(rows, width, BF16), shape(IDS, width, F32)],
    )
    out_received = swap(send)
    grads = finish(False, kept["first"][1:], out_state, [], [])
    out_received, grads = lax.optimization_barrier((out_received, grads))
    query_grad, *parts = kept["second"]
    key_grad, value_grad, gain_grad = finish(True, parts, out_received, [total], grads)
    if dp > 1:
        gain_grad = lax.psum_scatter(gain_grad, "dp", scatter_dimension=1, tiled=True)
    flat = (1, tokens, cols)
    return (query_grad.reshape(flat), key_grad.reshape(flat), value_grad.reshape(flat), gain_grad)


def solution(mesh):
    in_specs = (
        P("dp", "ctx", "tp"),
        P("dp", "ctx", "tp"),
        P("dp", "ctx", "tp"),
        P("dp", "ctx", "tp"),
        P("tp", None),
        P("dp", "ctx"),
    )
    out_specs = (P("dp", "ctx", "tp"), P("dp", "ctx", "tp"), P("dp", "ctx", "tp"), P("tp", "dp"))
    body = functools.partial(local, shards=mesh.shape["ctx"], dp=mesh.shape["dp"])
    return jax.shard_map(body, mesh=mesh, in_specs=in_specs, out_specs=out_specs, check_vma=False)
```

```python
import functools

import jax
import jax.numpy as jnp
from jax import lax
from jax.experimental import pallas as pl
from jax.experimental.pallas import tpu as pltpu
from jax.sharding import PartitionSpec as P

BLK = 128
EPSILON = 1e-06
CHIPS = 4
GROUP = 2 * CHIPS
IDS = 8
FIRST, LAST = 0, 1
F32, BF16 = jnp.float32, jnp.bfloat16


def dot(left, right, left_dim, right_dim):
    return lax.dot_general(
        left, right, (((left_dim,), (right_dim,)), ((), ())), preferred_element_type=F32
    )


def my_core():
    return lax.axis_index("ctx") % 2


def my_chip():
    return (lax.axis_index("ctx") // 2) % CHIPS


def one_doc(docs):
    return jnp.where(docs[0, 0] == docs[0, 1], 1.0, 0.0)


def column(docs, first_block, dtype):
    rows = lax.broadcasted_iota(jnp.int32, (2 * BLK, 1), 0)
    own = (rows < BLK) if first_block else (rows >= BLK)
    return jnp.where(own, 1.0, one_doc(docs)).astype(dtype)


def lower(table, both):
    rows = lax.broadcasted_iota(jnp.int32, (BLK, BLK), 0)
    cols = lax.broadcasted_iota(jnp.int32, (BLK, BLK), 1)
    keep = rows >= cols
    upper = jnp.where(keep, table[:BLK, :BLK], 0.0).astype(BF16)
    below = (table[BLK:, :BLK] * both).astype(BF16)
    right = jnp.where(keep, table[BLK:, BLK:], 0.0).astype(BF16)
    return upper, jnp.concatenate([below, right], 1)


def higher(table, both):
    rows = lax.broadcasted_iota(jnp.int32, (BLK, BLK), 0)
    cols = lax.broadcasted_iota(jnp.int32, (BLK, BLK), 1)
    keep = rows <= cols
    left = jnp.where(keep, table[:BLK, :BLK], 0.0).astype(BF16)
    above = (table[:BLK, BLK:] * both).astype(BF16)
    below = jnp.where(keep, table[BLK:, BLK:], 0.0).astype(BF16)
    return jnp.concatenate([left, above], 1), below


def times_lower(masked, values):
    upper, below = masked
    return jnp.concatenate([dot(upper, values[:BLK], 1, 0), dot(below, values, 1, 0)], 0)


def times_higher(masked, values):
    above, lower_right = masked
    return jnp.concatenate([dot(above, values, 1, 0), dot(lower_right, values[BLK:], 1, 0)], 0)


def write_ids(docs, out, rows, backward):
    first, last = docs[0, 0].astype(F32), docs[0, 1].astype(F32)
    if backward:
        first, last = -last, -first
    out[pl.ds(rows, IDS), :] = jnp.zeros((IDS, 128), F32)
    out[pl.ds(rows + FIRST, 1), :] = jnp.full((1, 128), first, F32)
    out[pl.ds(rows + LAST, 1), :] = jnp.full((1, 128), last, F32)


def wide(base, head):
    return pl.ds(pl.multiple_of((base + head) * 128, 128), 128)


def element(docs, key, value, out, first_col, half):
    weight = column(docs, False, BF16)
    write_ids(docs, out, half * 128, False)
    for head in range(half):
        at = wide(first_col, head)
        out[pl.ds(head * 128, 128), :] = dot(key[:, at] * weight, value[:, at], 0, 0)


def first_kernel(docs, key, value, out, key_own, value_own, docs_held, key_held, value_held, sems, *, half):
    core, rows = my_core(), half * 128
    far = pl.ds(pl.multiple_of((1 - core) * rows, rows), rows)
    own = pl.ds(pl.multiple_of(core * rows, rows), rows)
    copies = [
        pltpu.make_async_copy(docs, docs_held, sems.at[0]),
        pltpu.make_async_copy(key.at[:, far], key_held, sems.at[1]),
        pltpu.make_async_copy(value.at[:, far], value_held, sems.at[2]),
        pltpu.make_async_copy(key.at[:, own], key_own, sems.at[3]),
        pltpu.make_async_copy(value.at[:, own], value_own, sems.at[4]),
    ]
    for copy in copies:
        copy.start()
    for copy in copies[:3]:
        copy.wait()
    element(docs_held, key_held, value_held, out, 0, half)
    for copy in copies[3:]:
        copy.wait()


def second_kernel(docs, key, value, out, *, half):
    element(docs, key, value, out, 0, half)


def intra_kernel(docs, query, key, value, grad, own, message, *, half):
    both = one_doc(docs)
    tokens = query.shape[0]
    for other in (True, False):
        base = (1 - my_core() if other else my_core()) * half
        for head in range(half):
            full, cols = wide(base, head), pl.ds(head * 128, 128)
            q = query[:, full]
            scores = lower(dot(q, key[:, full], 1, 1), both)
            part = times_lower(scores, value[:, full])
            if other:
                message[pl.ds(0, tokens), cols] = q.astype(F32)
                message[pl.ds(tokens, tokens), cols] = grad[:, full].astype(F32)
                message[pl.ds(2 * tokens, tokens), cols] = part
            else:
                own[:, cols] = part


def channel_mean(table):
    high = table.astype(BF16)
    low = (table - high.astype(F32)).astype(BF16)
    return dot(jnp.concatenate([high, low], 1), jnp.full((256, 128), 1.0 / 128, BF16), 1, 0)


def attend(q, g, intra, state, gain, joined):
    inter = dot(q, state, 1, 0)
    attended = intra + jnp.concatenate([inter[:BLK], inter[BLK:] * joined], 0)
    inv_rms = lax.rsqrt(channel_mean(attended * attended) + EPSILON)
    scaled = g * gain
    normed = attended * inv_rms
    terms = jnp.sum(g * normed, 0, keepdims=True)
    mean = channel_mean(scaled * normed)
    attn = (inv_rms * (scaled - normed * mean)).astype(BF16)
    back = dot(q[:BLK], attn[:BLK], 0, 0) + dot(q[BLK:], attn[BLK:], 0, 0) * joined
    return attn, back, terms


def middle_kernel(
    docs, own, other, c0, c1, c2, c3, query, grad, intra, message, gain,
    up0, up1, up2, up3, back_own, back_other, attn_own, reply, state_own, *, half, size,
):
    rows, tokens, chunk = half * 128, query.shape[0], size // 128
    base = my_core() * half
    is_first = my_core() == 0
    own_first, own_last = row(own, rows, FIRST), row(own, rows, LAST)
    other_first, other_last = row(other, rows, FIRST), row(other, rows, LAST)
    keep_coming, keep_other, send_coming, send_own = spread_weights(
        is_first, own_first, own_last, other_first, other_last
    )
    own_joined, other_joined = match(own_first, own_last), match(other_first, other_last)
    for back, first, last in ((back_own, own_first, own_last), (back_other, other_first, other_last)):
        back[pl.ds(rows, IDS), :] = jnp.zeros((IDS, 128), F32)
        back[pl.ds(rows + FIRST, 1), :] = -last
        back[pl.ds(rows + LAST, 1), :] = -first
    first = jnp.minimum(own_first, other_first)
    last = jnp.maximum(own_last, other_last)
    own_weight, other_weight = match(own_first, first), match(other_first, first)
    ups = (up0, up1, up2, up3)
    for up in ups:
        up[pl.ds(size, 2 * IDS), :] = jnp.zeros((2 * IDS, 128), F32)
        up[pl.ds(size + FIRST, 1), :] = -last
        up[pl.ds(size + LAST, 1), :] = -first
    for turn, chip in enumerate((c0, c1, c2, c3)):
        for step in range(chunk):
            head = lax.bitwise_xor(my_chip(), turn) * chunk + step
            cols, full = wide(0, head), wide(base, head)
            coming = chip[pl.ds(step * 128, 128), :]
            state = (coming * keep_coming + other[cols, :] * keep_other).astype(BF16)
            state_own[cols, :] = state
            state_other = coming * send_coming + own[cols, :] * send_own
            reply[pl.ds(tokens, 128), cols] = state_other
            weights = gain[pl.ds(base + head, 1), :]
            attn, back, terms = attend(
                query[:, full], grad[:, full].astype(F32), intra[:, cols], state, weights, own_joined
            )
            attn_own[:, cols] = attn
            back_own[cols, :] = back
            attn, back_far, terms_far = attend(
                message[pl.ds(0, tokens), cols].astype(BF16),
                message[pl.ds(tokens, tokens), cols],
                message[pl.ds(2 * tokens, tokens), cols],
                state_other.astype(BF16),
                weights,
                other_joined,
            )
            reply[pl.ds(0, tokens), cols] = attn.astype(F32)
            back_other[cols, :] = back_far
            ups[turn][pl.ds(step * 128, 128), :] = back * own_weight + back_far * other_weight
            for up in ups:
                up[pl.ds(size + IDS + head, 1), :] = terms + terms_far


def within_kernel(docs, query, key, value, *refs, half, other):
    query_grad, key_part, value_part, held, sems = refs[-5:]
    tokens = query.shape[0]
    both = one_doc(docs)
    enter32 = column(docs, True, F32)
    base = (1 - my_core() if other else my_core()) * half
    copies = []
    for head in range(half):
        cols = pl.ds(head * 128, 128)
        full = wide(base, head)
        q, k, v = query[:, full], key[:, full], value[:, full]
        if other:
            a = refs[0][pl.ds(0, tokens), cols].astype(BF16)
            state = refs[0][pl.ds(tokens, 128), cols].astype(BF16)
        else:
            a, state = refs[0][:, cols], refs[1][cols, :]
        pair = lower(dot(a, v, 1, 1), both)
        cross = enter32 * dot(a, state, 1, 1)
        held[:, cols] = (cross + times_lower(pair, k)).astype(BF16)
        key_part[:, cols] = times_higher(higher(dot(v, a, 1, 1), both), q)
        value_part[:, cols] = times_higher(higher(dot(k, q, 1, 1), both), a)
        copies.append(pltpu.make_async_copy(held.at[:, cols], query_grad.at[:, full], sems.at[head]))
        copies[-1].start()
    for copy in copies:
        copy.wait()


def finish_kernel(docs, key, value, key_part, value_part, state, *refs, half, other):
    refs, (key_held, value_held, sems) = refs[:-3], refs[-3:]
    if other:
        refs, gain_grad = refs[:-1], refs[-1]
        for head in range(half):
            gain_grad[pl.ds(my_core() * half + head, 1), :] = refs[0][pl.ds(head, 1), :]
            gain_grad[pl.ds((1 - my_core()) * half + head, 1), :] = state[pl.ds(half * 128 + head, 1), :]
    key_grad, value_grad = refs[-2:]
    leave = column(docs, False, F32)
    base = (1 - my_core() if other else my_core()) * half
    copies = []
    for head in range(half):
        cols = pl.ds(head * 128, 128)
        full = wide(base, head)
        g = state[cols, :].astype(BF16)
        key_held[:, cols] = (key_part[:, cols] + leave * dot(value[:, full], g, 1, 1)).astype(BF16)
        value_held[:, cols] = (value_part[:, cols] + leave * dot(key[:, full], g, 1, 0)).astype(BF16)
        copies.append(pltpu.make_async_copy(key_held.at[:, cols], key_grad.at[:, full], sems.at[0, head]))
        copies.append(pltpu.make_async_copy(value_held.at[:, cols], value_grad.at[:, full], sems.at[1, head]))
        copies[-2].start()
        copies[-1].start()
    for copy in copies:
        copy.wait()


def row(ref, rows, which):
    return ref[pl.ds(rows + which, 1), :]


def match(left, right):
    return jnp.where(left == right, 1.0, 0.0)


def pair_kernel(docs, own, other, *outs, half, size):
    rows = half * 128
    first = jnp.minimum(row(own, rows, FIRST), row(other, rows, FIRST))
    last = jnp.maximum(row(own, rows, LAST), row(other, rows, LAST))
    own_weight = match(row(own, rows, LAST), last)
    other_weight = match(row(other, rows, LAST), last)
    for turn, out in enumerate(outs):
        owner = lax.bitwise_xor(my_chip(), turn)
        part = pl.ds(pl.multiple_of(owner * size, size), size)
        out[pl.ds(0, size), :] = own[part, :] * own_weight + other[part, :] * other_weight
        out[pl.ds(size, IDS), :] = jnp.zeros((IDS, 128), F32)
        out[pl.ds(size + FIRST, 1), :] = first
        out[pl.ds(size + LAST, 1), :] = last


def plane_kernel(docs, c0, c1, c2, c3, out, *gain, size):
    chips = (c0, c1, c2, c3)
    last = functools.reduce(jnp.maximum, [row(c, size, LAST) for c in chips])
    out[pl.ds(0, size), :] = sum(
        c[pl.ds(0, size), :] * match(row(c, size, LAST), last) for c in chips
    )
    out[pl.ds(size, IDS), :] = jnp.zeros((IDS, 128), F32)
    out[pl.ds(size + LAST, 1), :] = last
    if gain:
        gain[0][...] = sum(c[pl.ds(size + IDS, IDS), :] for c in chips)
        out[pl.ds(size + IDS, IDS), :] = gain[0][...]


def chain_kernel(docs, c0, c1, c2, c3, *refs, size, distances, planes):
    chips = (c0, c1, c2, c3)
    backward = distances[0] < 0
    others, outs = refs[: len(distances)], refs[-CHIPS:]
    place = [lax.bitwise_xor(my_chip(), turn) for turn in range(CHIPS)]
    my_plane = lax.axis_index("ctx") // GROUP
    first = functools.reduce(jnp.minimum, [row(c, size, FIRST) for c in chips])
    coming = jnp.zeros((size, 128), F32)
    for distance, other in zip(distances, others):
        source = my_plane - distance
        inside = (source >= 0) & (source < planes)
        weight = match(row(other, size, LAST), first) * jnp.where(inside, 1.0, 0.0)
        coming = coming + other[pl.ds(0, size), :] * weight
    if backward:
        gain, sums, outs = refs[len(distances)], refs[-1], refs[-1 - CHIPS : -1]
        sums[...] = gain[...] + sum(p[pl.ds(size + IDS, IDS), :] for p in others)
    for turn, out in enumerate(outs):
        mine = row(chips[turn], size, FIRST)
        total = coming * match(mine, first)
        for other in range(CHIPS):
            if other == turn:
                continue
            ahead = place[other] > place[turn] if backward else place[other] < place[turn]
            weight = match(row(chips[other], size, LAST), mine) * jnp.where(ahead, 1.0, 0.0)
            total = total + chips[other][pl.ds(0, size), :] * weight
        out[...] = total


def spread_weights(is_first, own_first, own_last, other_first, other_last):
    ones = jnp.ones((1, 128), F32)
    joins = match(own_first, other_first)
    return (
        jnp.where(is_first, ones, joins),
        jnp.where(is_first, 0.0 * ones, match(other_last, own_first)),
        jnp.where(is_first, joins, ones),
        jnp.where(is_first, match(own_last, other_first), 0.0 * ones),
    )


def spread_kernel(docs, own, other, c0, c1, c2, c3, sums, sums_near, send, keep, total, *, half, size):
    rows = half * 128
    keep_coming, keep_other, send_coming, send_own = spread_weights(
        my_core() == 1,
        row(own, rows, FIRST),
        row(own, rows, LAST),
        row(other, rows, FIRST),
        row(other, rows, LAST),
    )
    for turn, chip in enumerate((c0, c1, c2, c3)):
        owner = lax.bitwise_xor(my_chip(), turn)
        part = pl.ds(pl.multiple_of(owner * size, size), size)
        coming = chip[pl.ds(0, size), :]
        send[part, :] = coming * send_coming + own[part, :] * send_own
        keep[part, :] = (coming * keep_coming + other[part, :] * keep_other).astype(BF16)
    total[...] = sums[...] + sums_near[...]
    send[pl.ds(rows, IDS), :] = total[...]


def shape(rows, cols, dtype):
    return jax.ShapeDtypeStruct((rows, cols), dtype)


def call(kernel, docs, args, outs, flops=0, in_specs=None, out_specs=None, aliases=None, scratch=()):
    whole = pl.BlockSpec(memory_space=pltpu.VMEM)
    in_specs = in_specs or [None] * len(args)
    out_specs = out_specs or [None] * len(outs)
    moved = sum(a.size * a.dtype.itemsize for a in list(args) + list(outs))
    return pl.pallas_call(
        kernel,
        out_shape=outs,
        grid_spec=pltpu.PrefetchScalarGridSpec(
            num_scalar_prefetch=1,
            grid=(1,),
            in_specs=[spec or whole for spec in in_specs],
            out_specs=[spec or whole for spec in out_specs],
            scratch_shapes=scratch,
        ),
        input_output_aliases=aliases or {},
        cost_estimate=pl.CostEstimate(flops=flops, bytes_accessed=moved, transcendentals=0),
        compiler_params=pltpu.CompilerParams(vmem_limit_bytes=32 * 1024 * 1024),
    )(docs, *args)


def tie(value, *after):
    return lax.optimization_barrier((value, after))[0]


def local(queries, key_rows, value_rows, out_grad, norm_gain, doc_ids, *, shards, dp):
    tokens = queries.shape[1]
    heads, width = norm_gain.shape
    half = heads // 2
    rows, cols = half * width, heads * width
    size = rows // CHIPS
    query, key, value, grad = (
        a.reshape(tokens, cols) for a in (queries, key_rows, value_rows, out_grad)
    )
    planes = shards // GROUP
    any_place = pl.BlockSpec(memory_space=pl.ANY)

    def swap(value):
        return lax.ppermute(value, "ctx", [(i, i ^ 1) for i in range(shards)])

    def to_chips(values):
        return [values[0]] + [
            lax.ppermute(values[turn], "ctx", [(i, i ^ (2 * turn)) for i in range(shards)])
            for turn in (1, 2, 3)
        ]

    def around(value, distance):
        pairs = [(i, (i + distance * GROUP) % shards) for i in range(shards)]
        return lax.ppermute(value, "ctx", pairs)

    payload = shape(rows + IDS, width, F32)

    def chain(sent, backward, beside_up, beside_planes, beside_down):
        chunks = tie(to_chips(sent), beside_up(sent))
        plane, *gain = call(
            functools.partial(plane_kernel, size=size),
            doc_ids,
            chunks,
            [shape(size + (2 * IDS if backward else IDS), width, F32)]
            + ([shape(IDS, width, F32)] if backward else []),
        )
        distances = (-1, -2) if backward else (1, 2)
        others = [around(plane, distance) for distance in distances]
        others = tie(others, beside_planes(plane))
        sent = call(
            functools.partial(chain_kernel, size=size, distances=distances, planes=planes),
            doc_ids,
            [*chunks, *others, *gain],
            [shape(size, width, F32)] * CHIPS + ([shape(IDS, width, F32)] if backward else []),
        )
        return tie(to_chips(sent[:CHIPS]), beside_down(sent, *gain))

    def within(other, sources, into):
        spare = [] if into is None else [into]
        at = 3 + len(sources)
        return call(
            functools.partial(within_kernel, half=half, other=other),
            doc_ids,
            [query, key, value, *sources, *spare],
            [shape(tokens, cols, BF16), shape(tokens, rows, F32), shape(tokens, rows, F32)],
            flops=2 * half * tokens * width * (6 * tokens + width),
            in_specs=[None] * at + [any_place] * len(spare),
            out_specs=[any_place] + [None] * 2,
            aliases={1 + at: 0} if spare else None,
            scratch=[pltpu.VMEM((tokens, rows), BF16), pltpu.SemaphoreType.DMA((half,))],
        )

    def finish(other, parts, state, sums, into):
        return call(
            functools.partial(finish_kernel, half=half, other=other),
            doc_ids,
            [key, value, *parts, state, *sums, *into],
            [shape(tokens, cols, BF16)] * 2 + [shape(heads, width, F32)] * len(sums),
            flops=2 * half * tokens * width * 2 * width,
            in_specs=[None] * (5 + len(sums)) + [any_place] * len(into),
            out_specs=[any_place] * 2 + [None] * len(sums),
            aliases={7: 0, 8: 1} if into else None,
            scratch=[
                pltpu.VMEM((tokens, rows), BF16),
                pltpu.VMEM((tokens, rows), BF16),
                pltpu.SemaphoreType.DMA((2, half)),
            ],
        )

    hbm = pl.BlockSpec(memory_space=pltpu.HBM)
    vmem = pl.BlockSpec(memory_space=pltpu.VMEM)
    half_shape = shape(tokens, rows, BF16)
    states, key_own, value_own = pl.pallas_call(
        functools.partial(first_kernel, half=half),
        out_shape=[payload, half_shape, half_shape],
        in_specs=[hbm] * 3,
        out_specs=[vmem] * 3,
        scratch_shapes=[
            pltpu.SMEM(doc_ids.shape, jnp.int32),
            pltpu.VMEM(half_shape.shape, BF16),
            pltpu.VMEM(half_shape.shape, BF16),
            pltpu.SemaphoreType.DMA((5,)),
        ],
        cost_estimate=pl.CostEstimate(
            flops=2 * half * tokens * width * width, bytes_accessed=4 * tokens * rows * 2, transcendentals=0
        ),
        compiler_params=pltpu.CompilerParams(vmem_limit_bytes=32 * 1024 * 1024),
    )(*(pltpu.with_memory_space_constraint(x, pltpu.HBM) for x in (doc_ids, key, value)))
    received = swap(states)
    query, key, value, grad, doc_ids = tie((query, key, value, grad, doc_ids), states)
    (own,) = call(
        functools.partial(second_kernel, half=half),
        doc_ids,
        [key_own, value_own],
        [payload],
        flops=2 * half * tokens * width * width,
    )
    sent = call(
        functools.partial(pair_kernel, half=half, size=size),
        doc_ids,
        [own, received],
        [shape(size + IDS, width, F32)] * CHIPS,
    )

    kept = {}

    def intra(sent):
        kept["inside"], kept["message"] = call(
            functools.partial(intra_kernel, half=half),
            doc_ids,
            [tie(query, sent), key, value, grad],
            [shape(tokens, rows, F32), shape(3 * tokens, rows, F32)],
            flops=2 * heads * tokens * width * 2 * tokens,
        )
        return kept["inside"]

    def forward_message(plane):
        kept["message"] = swap(tie(kept["message"], plane))
        return []

    coming = chain(sent, False, intra, forward_message, lambda sent: [])
    *sent, back, back_other, attn, reply, state = call(
        functools.partial(middle_kernel, half=half, size=size),
        doc_ids,
        [own, received, *coming, query, grad, kept["inside"], kept["message"], norm_gain],
        [shape(size + 2 * IDS, width, F32)] * CHIPS
        + [payload, payload]
        + [shape(tokens, rows, BF16), shape(tokens + width, rows, F32), shape(rows, width, BF16)],
        flops=2 * heads * tokens * width * 2 * width,
    )

    def beside_up(sent):
        kept["first"] = within(False, [tie(attn, sent), state], None)
        return kept["first"]

    def beside_planes(plane):
        kept["reply"] = swap(tie(reply, plane))
        return []

    def beside_down(sent, gain):
        kept["sums"] = [sent[-1], around(tie(gain, sent), 1)]
        kept["second"] = within(True, [tie(kept["reply"], sent)], kept["first"][0])
        return kept["second"]

    coming = chain(sent, True, beside_up, beside_planes, beside_down)
    send, out_state, total = call(
        functools.partial(spread_kernel, half=half, size=size),
        doc_ids,
        [back, back_other, *coming, *kept["sums"]],
        [shape(rows + IDS, width, F32), shape(rows, width, BF16), shape(IDS, width, F32)],
    )
    out_received = swap(send)
    grads = finish(False, kept["first"][1:], out_state, [], [])
    out_received, grads = lax.optimization_barrier((out_received, grads))
    query_grad, *parts = kept["second"]
    key_grad, value_grad, gain_grad = finish(True, parts, out_received, [total], grads)
    if dp > 1:
        gain_grad = lax.psum_scatter(gain_grad, "dp", scatter_dimension=1, tiled=True)
    flat = (1, tokens, cols)
    return (query_grad.reshape(flat), key_grad.reshape(flat), value_grad.reshape(flat), gain_grad)


def solution(mesh):
    in_specs = (
        P("dp", "ctx", "tp"),
        P("dp", "ctx", "tp"),
        P("dp", "ctx", "tp"),
        P("dp", "ctx", "tp"),
        P("tp", None),
        P("dp", "ctx"),
    )
    out_specs = (P("dp", "ctx", "tp"), P("dp", "ctx", "tp"), P("dp", "ctx", "tp"), P("tp", "dp"))
    body = functools.partial(local, shards=mesh.shape["ctx"], dp=mesh.shape["dp"])
    return jax.shard_map(body, mesh=mesh, in_specs=in_specs, out_specs=out_specs, check_vma=False)
```

```python
import functools

import jax
import jax.numpy as jnp
from jax import lax
from jax.experimental import pallas as pl
from jax.experimental.pallas import tpu as pltpu
from jax.sharding import PartitionSpec as P

BLK = 128
EPSILON = 1e-06
CHIPS = 4
GROUP = 2 * CHIPS
IDS = 8
FIRST, LAST = 0, 1
F32, BF16 = jnp.float32, jnp.bfloat16


def dot(left, right, left_dim, right_dim):
    return lax.dot_general(
        left, right, (((left_dim,), (right_dim,)), ((), ())), preferred_element_type=F32
    )


def my_core():
    return lax.axis_index("ctx") % 2


def my_chip():
    return (lax.axis_index("ctx") // 2) % CHIPS


def one_doc(docs):
    return jnp.where(docs[0, 0] == docs[0, 1], 1.0, 0.0)


def column(docs, first_block, dtype):
    rows = lax.broadcasted_iota(jnp.int32, (2 * BLK, 1), 0)
    own = (rows < BLK) if first_block else (rows >= BLK)
    return jnp.where(own, 1.0, one_doc(docs)).astype(dtype)


def lower(table, both):
    rows = lax.broadcasted_iota(jnp.int32, (BLK, BLK), 0)
    cols = lax.broadcasted_iota(jnp.int32, (BLK, BLK), 1)
    keep = rows >= cols
    upper = jnp.where(keep, table[:BLK, :BLK], 0.0).astype(BF16)
    below = (table[BLK:, :BLK] * both).astype(BF16)
    right = jnp.where(keep, table[BLK:, BLK:], 0.0).astype(BF16)
    return upper, jnp.concatenate([below, right], 1)


def higher(table, both):
    rows = lax.broadcasted_iota(jnp.int32, (BLK, BLK), 0)
    cols = lax.broadcasted_iota(jnp.int32, (BLK, BLK), 1)
    keep = rows <= cols
    left = jnp.where(keep, table[:BLK, :BLK], 0.0).astype(BF16)
    above = (table[:BLK, BLK:] * both).astype(BF16)
    below = jnp.where(keep, table[BLK:, BLK:], 0.0).astype(BF16)
    return jnp.concatenate([left, above], 1), below


def times_lower(masked, values):
    upper, below = masked
    return jnp.concatenate([dot(upper, values[:BLK], 1, 0), dot(below, values, 1, 0)], 0)


def times_higher(masked, values):
    above, lower_right = masked
    return jnp.concatenate([dot(above, values, 1, 0), dot(lower_right, values[BLK:], 1, 0)], 0)


def write_ids(docs, out, rows, backward):
    first, last = docs[0, 0].astype(F32), docs[0, 1].astype(F32)
    if backward:
        first, last = -last, -first
    out[pl.ds(rows, IDS), :] = jnp.zeros((IDS, 128), F32)
    out[pl.ds(rows + FIRST, 1), :] = jnp.full((1, 128), first, F32)
    out[pl.ds(rows + LAST, 1), :] = jnp.full((1, 128), last, F32)


def wide(base, head):
    return pl.ds(pl.multiple_of((base + head) * 128, 128), 128)


def batches(total, most):
    most = most if total % most == 0 else 1
    return [range(start, start + most) for start in range(0, total, most)]


def element(docs, key, value, out, first_col, half):
    weight = column(docs, False, BF16)
    write_ids(docs, out, half * 128, False)
    for heads in batches(half, 4):
        columns = [wide(first_col, head) for head in heads]
        states = [dot(key[:, at] * weight, value[:, at], 0, 0) for at in columns]
        for head, state in zip(heads, states):
            out[pl.ds(head * 128, 128), :] = state


def first_kernel(docs, key, value, out, key_own, value_own, docs_held, key_held, value_held, sems, *, half):
    core, rows = my_core(), half * 128
    far = pl.ds(pl.multiple_of((1 - core) * rows, rows), rows)
    own = pl.ds(pl.multiple_of(core * rows, rows), rows)
    copies = [
        pltpu.make_async_copy(docs, docs_held, sems.at[0]),
        pltpu.make_async_copy(key.at[:, far], key_held, sems.at[1]),
        pltpu.make_async_copy(value.at[:, far], value_held, sems.at[2]),
        pltpu.make_async_copy(key.at[:, own], key_own, sems.at[3]),
        pltpu.make_async_copy(value.at[:, own], value_own, sems.at[4]),
    ]
    for copy in copies:
        copy.start()
    for copy in copies[:3]:
        copy.wait()
    element(docs_held, key_held, value_held, out, 0, half)
    for copy in copies[3:]:
        copy.wait()


def second_kernel(docs, key, value, out, *, half):
    element(docs, key, value, out, 0, half)


def intra_kernel(docs, query, key, value, grad, own, message, *, half):
    both = one_doc(docs)
    tokens = query.shape[0]
    for other in (True, False):
        base = (1 - my_core() if other else my_core()) * half
        for heads in batches(half, 2):
            results = []
            for head in heads:
                full = wide(base, head)
                q = query[:, full]
                scores = lower(dot(q, key[:, full], 1, 1), both)
                part = times_lower(scores, value[:, full])
                results.append((q.astype(F32), grad[:, full].astype(F32), part) if other else (part,))
            for head, parts in zip(heads, results):
                cols = pl.ds(head * 128, 128)
                if other:
                    for at, part in enumerate(parts):
                        message[pl.ds(at * tokens, tokens), cols] = part
                else:
                    own[:, cols] = parts[0]


def attend(q, g, intra, state, gain, joined):
    inter = dot(q, state, 1, 0)
    attended = intra + jnp.concatenate([inter[:BLK], inter[BLK:] * joined], 0)
    inv_rms = lax.rsqrt(jnp.mean(attended * attended, -1, keepdims=True) + EPSILON)
    scaled = g * gain
    normed = attended * inv_rms
    terms = jnp.sum(g * normed, 0, keepdims=True)
    mean = jnp.mean(scaled * normed, -1, keepdims=True)
    attn = (inv_rms * (scaled - normed * mean)).astype(BF16)
    back = dot(q[:BLK], attn[:BLK], 0, 0) + dot(q[BLK:], attn[BLK:], 0, 0) * joined
    return attn, back, terms


def middle_kernel(
    docs, own, other, c0, c1, c2, c3, query, grad, intra, message, gain,
    up0, up1, up2, up3, back_own, back_other, attn_own, reply, state_own, *, half, size,
):
    rows, tokens, chunk = half * 128, query.shape[0], size // 128
    base = my_core() * half
    is_first = my_core() == 0
    own_first, own_last = row(own, rows, FIRST), row(own, rows, LAST)
    other_first, other_last = row(other, rows, FIRST), row(other, rows, LAST)
    keep_coming, keep_other, send_coming, send_own = spread_weights(
        is_first, own_first, own_last, other_first, other_last
    )
    own_joined, other_joined = match(own_first, own_last), match(other_first, other_last)
    for back, first, last in ((back_own, own_first, own_last), (back_other, other_first, other_last)):
        back[pl.ds(rows, IDS), :] = jnp.zeros((IDS, 128), F32)
        back[pl.ds(rows + FIRST, 1), :] = -last
        back[pl.ds(rows + LAST, 1), :] = -first
    first = jnp.minimum(own_first, other_first)
    last = jnp.maximum(own_last, other_last)
    own_weight, other_weight = match(own_first, first), match(other_first, first)
    ups = (up0, up1, up2, up3)
    for up in ups:
        up[pl.ds(size, 2 * IDS), :] = jnp.zeros((2 * IDS, 128), F32)
        up[pl.ds(size + FIRST, 1), :] = -last
        up[pl.ds(size + LAST, 1), :] = -first
    for turn, chip in enumerate((c0, c1, c2, c3)):
        results = []
        for step in range(chunk):
            head = lax.bitwise_xor(my_chip(), turn) * chunk + step
            cols, full = wide(0, head), wide(base, head)
            coming = chip[pl.ds(step * 128, 128), :]
            state = (coming * keep_coming + other[cols, :] * keep_other).astype(BF16)
            state_other = coming * send_coming + own[cols, :] * send_own
            weights = gain[pl.ds(base + head, 1), :]
            near = attend(
                query[:, full], grad[:, full].astype(F32), intra[:, cols], state, weights, own_joined
            )
            far = attend(
                message[pl.ds(0, tokens), cols].astype(BF16),
                message[pl.ds(tokens, tokens), cols],
                message[pl.ds(2 * tokens, tokens), cols],
                state_other.astype(BF16),
                weights,
                other_joined,
            )
            results.append((head, cols, state, state_other, near, far))
        for step, (head, cols, state, state_other, near, far) in enumerate(results):
            attn, back, terms = near
            attn_far, back_far, terms_far = far
            state_own[cols, :] = state
            reply[pl.ds(tokens, 128), cols] = state_other
            attn_own[:, cols] = attn
            back_own[cols, :] = back
            reply[pl.ds(0, tokens), cols] = attn_far.astype(F32)
            back_other[cols, :] = back_far
            ups[turn][pl.ds(step * 128, 128), :] = back * own_weight + back_far * other_weight
            for up in ups:
                up[pl.ds(size + IDS + head, 1), :] = terms + terms_far


def within_kernel(docs, query, key, value, *refs, half, other):
    query_grad, key_part, value_part, held, sems = refs[-5:]
    tokens = query.shape[0]
    both = one_doc(docs)
    enter32 = column(docs, True, F32)
    base = (1 - my_core() if other else my_core()) * half
    copies = []
    for heads in batches(half, 2):
        results = []
        for head in heads:
            cols, full = pl.ds(head * 128, 128), wide(base, head)
            q, k, v = query[:, full], key[:, full], value[:, full]
            if other:
                a = refs[0][pl.ds(0, tokens), cols].astype(BF16)
                state = refs[0][pl.ds(tokens, 128), cols].astype(BF16)
            else:
                a, state = refs[0][:, cols], refs[1][cols, :]
            pair = lower(dot(a, v, 1, 1), both)
            cross = enter32 * dot(a, state, 1, 1)
            results.append(
                (
                    (cross + times_lower(pair, k)).astype(BF16),
                    times_higher(higher(dot(v, a, 1, 1), both), q),
                    times_higher(higher(dot(k, q, 1, 1), both), a),
                )
            )
        for head, (query_part, key_term, value_term) in zip(heads, results):
            cols, full = pl.ds(head * 128, 128), wide(base, head)
            held[:, cols] = query_part
            copies.append(pltpu.make_async_copy(held.at[:, cols], query_grad.at[:, full], sems.at[head]))
            copies[-1].start()
            key_part[:, cols] = key_term
            value_part[:, cols] = value_term
    for copy in copies:
        copy.wait()


def finish_kernel(docs, key, value, key_part, value_part, state, *refs, half, other):
    refs, (key_held, value_held, sems) = refs[:-3], refs[-3:]
    if other:
        refs, gain_grad = refs[:-1], refs[-1]
        for head in range(half):
            gain_grad[pl.ds(my_core() * half + head, 1), :] = refs[0][pl.ds(head, 1), :]
            gain_grad[pl.ds((1 - my_core()) * half + head, 1), :] = state[pl.ds(half * 128 + head, 1), :]
    key_grad, value_grad = refs[-2:]
    leave = column(docs, False, F32)
    base = (1 - my_core() if other else my_core()) * half
    copies = []
    for heads in batches(half, 4):
        results = []
        for head in heads:
            cols, full = pl.ds(head * 128, 128), wide(base, head)
            g = state[cols, :].astype(BF16)
            results.append(
                (
                    (key_part[:, cols] + leave * dot(value[:, full], g, 1, 1)).astype(BF16),
                    (value_part[:, cols] + leave * dot(key[:, full], g, 1, 0)).astype(BF16),
                )
            )
        for head, (key_sum, value_sum) in zip(heads, results):
            cols, full = pl.ds(head * 128, 128), wide(base, head)
            key_held[:, cols] = key_sum
            value_held[:, cols] = value_sum
            copies.append(pltpu.make_async_copy(key_held.at[:, cols], key_grad.at[:, full], sems.at[0, head]))
            copies.append(pltpu.make_async_copy(value_held.at[:, cols], value_grad.at[:, full], sems.at[1, head]))
            copies[-2].start()
            copies[-1].start()
    for copy in copies:
        copy.wait()


def row(ref, rows, which):
    return ref[pl.ds(rows + which, 1), :]


def match(left, right):
    return jnp.where(left == right, 1.0, 0.0)


def pair_kernel(docs, own, other, *outs, half, size):
    rows = half * 128
    first = jnp.minimum(row(own, rows, FIRST), row(other, rows, FIRST))
    last = jnp.maximum(row(own, rows, LAST), row(other, rows, LAST))
    own_weight = match(row(own, rows, LAST), last)
    other_weight = match(row(other, rows, LAST), last)
    for turn, out in enumerate(outs):
        owner = lax.bitwise_xor(my_chip(), turn)
        part = pl.ds(pl.multiple_of(owner * size, size), size)
        out[pl.ds(0, size), :] = own[part, :] * own_weight + other[part, :] * other_weight
        out[pl.ds(size, IDS), :] = jnp.zeros((IDS, 128), F32)
        out[pl.ds(size + FIRST, 1), :] = first
        out[pl.ds(size + LAST, 1), :] = last


def plane_kernel(docs, c0, c1, c2, c3, out, *gain, size):
    chips = (c0, c1, c2, c3)
    last = functools.reduce(jnp.maximum, [row(c, size, LAST) for c in chips])
    out[pl.ds(0, size), :] = sum(
        c[pl.ds(0, size), :] * match(row(c, size, LAST), last) for c in chips
    )
    out[pl.ds(size, IDS), :] = jnp.zeros((IDS, 128), F32)
    out[pl.ds(size + LAST, 1), :] = last
    if gain:
        gain[0][...] = sum(c[pl.ds(size + IDS, IDS), :] for c in chips)
        out[pl.ds(size + IDS, IDS), :] = gain[0][...]


def chain_kernel(docs, c0, c1, c2, c3, *refs, size, distances, planes):
    chips = (c0, c1, c2, c3)
    backward = distances[0] < 0
    others, outs = refs[: len(distances)], refs[-CHIPS:]
    place = [lax.bitwise_xor(my_chip(), turn) for turn in range(CHIPS)]
    my_plane = lax.axis_index("ctx") // GROUP
    first = functools.reduce(jnp.minimum, [row(c, size, FIRST) for c in chips])
    coming = jnp.zeros((size, 128), F32)
    for distance, other in zip(distances, others):
        source = my_plane - distance
        inside = (source >= 0) & (source < planes)
        weight = match(row(other, size, LAST), first) * jnp.where(inside, 1.0, 0.0)
        coming = coming + other[pl.ds(0, size), :] * weight
    if backward:
        gain, sums, outs = refs[len(distances)], refs[-1], refs[-1 - CHIPS : -1]
        sums[...] = gain[...] + sum(p[pl.ds(size + IDS, IDS), :] for p in others)
    for turn, out in enumerate(outs):
        mine = row(chips[turn], size, FIRST)
        total = coming * match(mine, first)
        for other in range(CHIPS):
            if other == turn:
                continue
            ahead = place[other] > place[turn] if backward else place[other] < place[turn]
            weight = match(row(chips[other], size, LAST), mine) * jnp.where(ahead, 1.0, 0.0)
            total = total + chips[other][pl.ds(0, size), :] * weight
        out[...] = total


def spread_weights(is_first, own_first, own_last, other_first, other_last):
    ones = jnp.ones((1, 128), F32)
    joins = match(own_first, other_first)
    return (
        jnp.where(is_first, ones, joins),
        jnp.where(is_first, 0.0 * ones, match(other_last, own_first)),
        jnp.where(is_first, joins, ones),
        jnp.where(is_first, match(own_last, other_first), 0.0 * ones),
    )


def spread_kernel(docs, own, other, c0, c1, c2, c3, sums, sums_near, send, keep, total, *, half, size):
    rows = half * 128
    keep_coming, keep_other, send_coming, send_own = spread_weights(
        my_core() == 1,
        row(own, rows, FIRST),
        row(own, rows, LAST),
        row(other, rows, FIRST),
        row(other, rows, LAST),
    )
    for turn, chip in enumerate((c0, c1, c2, c3)):
        owner = lax.bitwise_xor(my_chip(), turn)
        part = pl.ds(pl.multiple_of(owner * size, size), size)
        coming = chip[pl.ds(0, size), :]
        send[part, :] = coming * send_coming + own[part, :] * send_own
        keep[part, :] = (coming * keep_coming + other[part, :] * keep_other).astype(BF16)
    total[...] = sums[...] + sums_near[...]
    send[pl.ds(rows, IDS), :] = total[...]


def shape(rows, cols, dtype):
    return jax.ShapeDtypeStruct((rows, cols), dtype)


def call(kernel, docs, args, outs, flops=0, in_specs=None, out_specs=None, aliases=None, scratch=()):
    whole = pl.BlockSpec(memory_space=pltpu.VMEM)
    in_specs = in_specs or [None] * len(args)
    out_specs = out_specs or [None] * len(outs)
    moved = sum(a.size * a.dtype.itemsize for a in list(args) + list(outs))
    return pl.pallas_call(
        kernel,
        out_shape=outs,
        grid_spec=pltpu.PrefetchScalarGridSpec(
            num_scalar_prefetch=1,
            grid=(1,),
            in_specs=[spec or whole for spec in in_specs],
            out_specs=[spec or whole for spec in out_specs],
            scratch_shapes=scratch,
        ),
        input_output_aliases=aliases or {},
        cost_estimate=pl.CostEstimate(flops=flops, bytes_accessed=moved, transcendentals=0),
        compiler_params=pltpu.CompilerParams(vmem_limit_bytes=32 * 1024 * 1024),
    )(docs, *args)


def tie(value, *after):
    return lax.optimization_barrier((value, after))[0]


def local(queries, key_rows, value_rows, out_grad, norm_gain, doc_ids, *, shards, dp):
    tokens = queries.shape[1]
    heads, width = norm_gain.shape
    half = heads // 2
    rows, cols = half * width, heads * width
    size = rows // CHIPS
    query, key, value, grad = (
        a.reshape(tokens, cols) for a in (queries, key_rows, value_rows, out_grad)
    )
    planes = shards // GROUP
    any_place = pl.BlockSpec(memory_space=pl.ANY)

    def swap(value):
        return lax.ppermute(value, "ctx", [(i, i ^ 1) for i in range(shards)])

    def to_chips(values):
        return [values[0]] + [
            lax.ppermute(values[turn], "ctx", [(i, i ^ (2 * turn)) for i in range(shards)])
            for turn in (1, 2, 3)
        ]

    def around(value, distance):
        pairs = [(i, (i + distance * GROUP) % shards) for i in range(shards)]
        return lax.ppermute(value, "ctx", pairs)

    payload = shape(rows + IDS, width, F32)

    def chain(sent, backward, beside_up, beside_planes, beside_down):
        chunks = tie(to_chips(sent), beside_up(sent))
        plane, *gain = call(
            functools.partial(plane_kernel, size=size),
            doc_ids,
            chunks,
            [shape(size + (2 * IDS if backward else IDS), width, F32)]
            + ([shape(IDS, width, F32)] if backward else []),
        )
        distances = (-1, -2) if backward else (1, 2)
        others = [around(plane, distance) for distance in distances]
        others = tie(others, beside_planes(plane))
        sent = call(
            functools.partial(chain_kernel, size=size, distances=distances, planes=planes),
            doc_ids,
            [*chunks, *others, *gain],
            [shape(size, width, F32)] * CHIPS + ([shape(IDS, width, F32)] if backward else []),
        )
        return tie(to_chips(sent[:CHIPS]), beside_down(sent, *gain))

    def within(other, sources, into):
        spare = [] if into is None else [into]
        at = 3 + len(sources)
        return call(
            functools.partial(within_kernel, half=half, other=other),
            doc_ids,
            [query, key, value, *sources, *spare],
            [shape(tokens, cols, BF16), shape(tokens, rows, F32), shape(tokens, rows, F32)],
            flops=2 * half * tokens * width * (6 * tokens + width),
            in_specs=[None] * at + [any_place] * len(spare),
            out_specs=[any_place] + [None] * 2,
            aliases={1 + at: 0} if spare else None,
            scratch=[pltpu.VMEM((tokens, rows), BF16), pltpu.SemaphoreType.DMA((half,))],
        )

    def finish(other, parts, state, sums, into):
        return call(
            functools.partial(finish_kernel, half=half, other=other),
            doc_ids,
            [key, value, *parts, state, *sums, *into],
            [shape(tokens, cols, BF16)] * 2 + [shape(heads, width, F32)] * len(sums),
            flops=2 * half * tokens * width * 2 * width,
            in_specs=[None] * (5 + len(sums)) + [any_place] * len(into),
            out_specs=[any_place] * 2 + [None] * len(sums),
            aliases={7: 0, 8: 1} if into else None,
            scratch=[
                pltpu.VMEM((tokens, rows), BF16),
                pltpu.VMEM((tokens, rows), BF16),
                pltpu.SemaphoreType.DMA((2, half)),
            ],
        )

    hbm = pl.BlockSpec(memory_space=pltpu.HBM)
    vmem = pl.BlockSpec(memory_space=pltpu.VMEM)
    half_shape = shape(tokens, rows, BF16)
    states, key_own, value_own = pl.pallas_call(
        functools.partial(first_kernel, half=half),
        out_shape=[payload, half_shape, half_shape],
        in_specs=[hbm] * 3,
        out_specs=[vmem] * 3,
        scratch_shapes=[
            pltpu.SMEM(doc_ids.shape, jnp.int32),
            pltpu.VMEM(half_shape.shape, BF16),
            pltpu.VMEM(half_shape.shape, BF16),
            pltpu.SemaphoreType.DMA((5,)),
        ],
        cost_estimate=pl.CostEstimate(
            flops=2 * half * tokens * width * width, bytes_accessed=4 * tokens * rows * 2, transcendentals=0
        ),
        compiler_params=pltpu.CompilerParams(vmem_limit_bytes=32 * 1024 * 1024),
    )(*(pltpu.with_memory_space_constraint(x, pltpu.HBM) for x in (doc_ids, key, value)))
    received = swap(states)
    query, key, value, grad, doc_ids = tie((query, key, value, grad, doc_ids), states)
    (own,) = call(
        functools.partial(second_kernel, half=half),
        doc_ids,
        [key_own, value_own],
        [payload],
        flops=2 * half * tokens * width * width,
    )
    sent = call(
        functools.partial(pair_kernel, half=half, size=size),
        doc_ids,
        [own, received],
        [shape(size + IDS, width, F32)] * CHIPS,
    )

    kept = {}

    def intra(sent):
        kept["inside"], kept["message"] = call(
            functools.partial(intra_kernel, half=half),
            doc_ids,
            [tie(query, sent), key, value, grad],
            [shape(tokens, rows, F32), shape(3 * tokens, rows, F32)],
            flops=2 * heads * tokens * width * 2 * tokens,
        )
        return kept["inside"]

    def forward_message(plane):
        kept["message"] = swap(tie(kept["message"], plane))
        return []

    coming = chain(sent, False, intra, forward_message, lambda sent: [])
    *sent, back, back_other, attn, reply, state = call(
        functools.partial(middle_kernel, half=half, size=size),
        doc_ids,
        [own, received, *coming, query, grad, kept["inside"], kept["message"], norm_gain],
        [shape(size + 2 * IDS, width, F32)] * CHIPS
        + [payload, payload]
        + [shape(tokens, rows, BF16), shape(tokens + width, rows, F32), shape(rows, width, BF16)],
        flops=2 * heads * tokens * width * 2 * width,
    )

    def beside_up(sent):
        kept["first"] = within(False, [tie(attn, sent), state], None)
        return kept["first"]

    def beside_planes(plane):
        kept["reply"] = swap(tie(reply, plane))
        return []

    def beside_down(sent, gain):
        kept["sums"] = [sent[-1], around(tie(gain, sent), 1)]
        kept["second"] = within(True, [tie(kept["reply"], sent)], kept["first"][0])
        return kept["second"]

    coming = chain(sent, True, beside_up, beside_planes, beside_down)
    send, out_state, total = call(
        functools.partial(spread_kernel, half=half, size=size),
        doc_ids,
        [back, back_other, *coming, *kept["sums"]],
        [shape(rows + IDS, width, F32), shape(rows, width, BF16), shape(IDS, width, F32)],
    )
    out_received = swap(send)
    grads = finish(False, kept["first"][1:], out_state, [], [])
    out_received, grads = lax.optimization_barrier((out_received, grads))
    query_grad, *parts = kept["second"]
    key_grad, value_grad, gain_grad = finish(True, parts, out_received, [total], grads)
    if dp > 1:
        gain_grad = lax.psum_scatter(gain_grad, "dp", scatter_dimension=1, tiled=True)
    flat = (1, tokens, cols)
    return (query_grad.reshape(flat), key_grad.reshape(flat), value_grad.reshape(flat), gain_grad)


def solution(mesh):
    in_specs = (
        P("dp", "ctx", "tp"),
        P("dp", "ctx", "tp"),
        P("dp", "ctx", "tp"),
        P("dp", "ctx", "tp"),
        P("tp", None),
        P("dp", "ctx"),
    )
    out_specs = (P("dp", "ctx", "tp"), P("dp", "ctx", "tp"), P("dp", "ctx", "tp"), P("tp", "dp"))
    body = functools.partial(local, shards=mesh.shape["ctx"], dp=mesh.shape["dp"])
    return jax.shard_map(body, mesh=mesh, in_specs=in_specs, out_specs=out_specs, check_vma=False)
```

```python
import functools

import jax
import jax.numpy as jnp
from jax import lax
from jax.experimental import pallas as pl
from jax.experimental.pallas import tpu as pltpu
from jax.sharding import PartitionSpec as P

BLK = 128
EPSILON = 1e-06
CHIPS = 4
GROUP = 2 * CHIPS
IDS = 8
FIRST, LAST = 0, 1
F32, BF16 = jnp.float32, jnp.bfloat16


def dot(left, right, left_dim, right_dim):
    return lax.dot_general(
        left, right, (((left_dim,), (right_dim,)), ((), ())), preferred_element_type=F32
    )


def my_core():
    return lax.axis_index("ctx") % 2


def my_chip():
    return (lax.axis_index("ctx") // 2) % CHIPS


def one_doc(docs):
    return jnp.where(docs[0, 0] == docs[0, 1], 1.0, 0.0)


def column(docs, first_block, dtype):
    rows = lax.broadcasted_iota(jnp.int32, (2 * BLK, 1), 0)
    own = (rows < BLK) if first_block else (rows >= BLK)
    return jnp.where(own, 1.0, one_doc(docs)).astype(dtype)


def lower(table, both):
    rows = lax.broadcasted_iota(jnp.int32, (BLK, BLK), 0)
    cols = lax.broadcasted_iota(jnp.int32, (BLK, BLK), 1)
    keep = rows >= cols
    upper = jnp.where(keep, table[:BLK, :BLK], 0.0).astype(BF16)
    below = (table[BLK:, :BLK] * both).astype(BF16)
    right = jnp.where(keep, table[BLK:, BLK:], 0.0).astype(BF16)
    return upper, jnp.concatenate([below, right], 1)


def higher(table, both):
    rows = lax.broadcasted_iota(jnp.int32, (BLK, BLK), 0)
    cols = lax.broadcasted_iota(jnp.int32, (BLK, BLK), 1)
    keep = rows <= cols
    left = jnp.where(keep, table[:BLK, :BLK], 0.0).astype(BF16)
    above = (table[:BLK, BLK:] * both).astype(BF16)
    below = jnp.where(keep, table[BLK:, BLK:], 0.0).astype(BF16)
    return jnp.concatenate([left, above], 1), below


def times_lower(masked, values):
    upper, below = masked
    return jnp.concatenate([dot(upper, values[:BLK], 1, 0), dot(below, values, 1, 0)], 0)


def times_higher(masked, values):
    above, lower_right = masked
    return jnp.concatenate([dot(above, values, 1, 0), dot(lower_right, values[BLK:], 1, 0)], 0)


def write_ids(docs, out, rows, backward):
    first, last = docs[0, 0].astype(F32), docs[0, 1].astype(F32)
    if backward:
        first, last = -last, -first
    out[pl.ds(rows, IDS), :] = jnp.zeros((IDS, 128), F32)
    out[pl.ds(rows + FIRST, 1), :] = jnp.full((1, 128), first, F32)
    out[pl.ds(rows + LAST, 1), :] = jnp.full((1, 128), last, F32)


def wide(base, head):
    return pl.ds(pl.multiple_of((base + head) * 128, 128), 128)


def batches(total, most):
    most = most if total % most == 0 else 1
    return [range(start, start + most) for start in range(0, total, most)]


def element(docs, key, value, out, first_col, half):
    weight = column(docs, False, BF16)
    write_ids(docs, out, half * 128, False)
    for heads in batches(half, 4):
        columns = [wide(first_col, head) for head in heads]
        states = [dot(key[:, at] * weight, value[:, at], 0, 0) for at in columns]
        for head, state in zip(heads, states):
            out[pl.ds(head * 128, 128), :] = state


def first_kernel(docs, key, value, out, key_own, value_own, docs_held, key_held, value_held, sems, *, half):
    core, rows = my_core(), half * 128
    far = pl.ds(pl.multiple_of((1 - core) * rows, rows), rows)
    own = pl.ds(pl.multiple_of(core * rows, rows), rows)
    copies = [
        pltpu.make_async_copy(docs, docs_held, sems.at[0]),
        pltpu.make_async_copy(key.at[:, far], key_held, sems.at[1]),
        pltpu.make_async_copy(value.at[:, far], value_held, sems.at[2]),
        pltpu.make_async_copy(key.at[:, own], key_own, sems.at[3]),
        pltpu.make_async_copy(value.at[:, own], value_own, sems.at[4]),
    ]
    for copy in copies:
        copy.start()
    for copy in copies[:3]:
        copy.wait()
    element(docs_held, key_held, value_held, out, 0, half)
    for copy in copies[3:]:
        copy.wait()


def second_kernel(docs, key, value, out, *, half):
    element(docs, key, value, out, 0, half)


def intra_kernel(docs, query, key, value, grad, own, message, *, half):
    both = one_doc(docs)
    tokens = query.shape[0]
    for other in (True, False):
        base = (1 - my_core() if other else my_core()) * half
        for heads in batches(half, 2):
            results = []
            for head in heads:
                full = wide(base, head)
                q = query[:, full]
                scores = lower(dot(q, key[:, full], 1, 1), both)
                part = times_lower(scores, value[:, full])
                results.append((q.astype(F32), grad[:, full].astype(F32), part) if other else (part,))
            for head, parts in zip(heads, results):
                cols = pl.ds(head * 128, 128)
                if other:
                    for at, part in enumerate(parts):
                        message[pl.ds(at * tokens, tokens), cols] = part
                else:
                    own[:, cols] = parts[0]


def attend(q, g, intra, state, gain, joined):
    inter = dot(q, state, 1, 0)
    attended = intra + jnp.concatenate([inter[:BLK], inter[BLK:] * joined], 0)
    inv_rms = lax.rsqrt(jnp.mean(attended * attended, -1, keepdims=True) + EPSILON)
    scaled = g * gain
    normed = attended * inv_rms
    terms = jnp.sum(g * normed, 0, keepdims=True)
    mean = jnp.mean(scaled * normed, -1, keepdims=True)
    attn = (inv_rms * (scaled - normed * mean)).astype(BF16)
    back = dot(q[:BLK], attn[:BLK], 0, 0) + dot(q[BLK:], attn[BLK:], 0, 0) * joined
    return attn, back, terms


def middle_kernel(
    docs, own, other, c0, c1, c2, c3, query, grad, intra, message, gain,
    up0, up1, up2, up3, back_own, back_other, attn_own, reply, state_own, *, half, size,
):
    rows, tokens, chunk = half * 128, query.shape[0], size // 128
    base = my_core() * half
    is_first = my_core() == 0
    own_first, own_last = row(own, rows, FIRST), row(own, rows, LAST)
    other_first, other_last = row(other, rows, FIRST), row(other, rows, LAST)
    keep_coming, keep_other, send_coming, send_own = spread_weights(
        is_first, own_first, own_last, other_first, other_last
    )
    own_joined, other_joined = match(own_first, own_last), match(other_first, other_last)
    for back, first, last in ((back_own, own_first, own_last), (back_other, other_first, other_last)):
        back[pl.ds(rows, IDS), :] = jnp.zeros((IDS, 128), F32)
        back[pl.ds(rows + FIRST, 1), :] = -last
        back[pl.ds(rows + LAST, 1), :] = -first
    first = jnp.minimum(own_first, other_first)
    last = jnp.maximum(own_last, other_last)
    own_weight, other_weight = match(own_first, first), match(other_first, first)
    ups = (up0, up1, up2, up3)
    for up in ups:
        up[pl.ds(size, 2 * IDS), :] = jnp.zeros((2 * IDS, 128), F32)
        up[pl.ds(size + FIRST, 1), :] = -last
        up[pl.ds(size + LAST, 1), :] = -first
    for turn, chip in enumerate((c0, c1, c2, c3)):
        results = []
        for step in range(chunk):
            head = lax.bitwise_xor(my_chip(), turn) * chunk + step
            cols, full = wide(0, head), wide(base, head)
            coming = chip[pl.ds(step * 128, 128), :]
            state = (coming * keep_coming + other[cols, :] * keep_other).astype(BF16)
            state_other = coming * send_coming + own[cols, :] * send_own
            weights = gain[pl.ds(base + head, 1), :]
            near = attend(
                query[:, full], grad[:, full].astype(F32), intra[:, cols], state, weights, own_joined
            )
            far = attend(
                message[pl.ds(0, tokens), cols].astype(BF16),
                message[pl.ds(tokens, tokens), cols],
                message[pl.ds(2 * tokens, tokens), cols],
                state_other.astype(BF16),
                weights,
                other_joined,
            )
            results.append((head, cols, state, state_other, near, far))
        for step, (head, cols, state, state_other, near, far) in enumerate(results):
            attn, back, terms = near
            attn_far, back_far, terms_far = far
            state_own[cols, :] = state
            reply[pl.ds(tokens, 128), cols] = state_other
            attn_own[:, cols] = attn
            back_own[cols, :] = back
            reply[pl.ds(0, tokens), cols] = attn_far.astype(F32)
            back_other[cols, :] = back_far
            ups[turn][pl.ds(step * 128, 128), :] = back * own_weight + back_far * other_weight
            for up in ups:
                up[pl.ds(size + IDS + head, 1), :] = terms + terms_far


def within_kernel(docs, query, key, value, *refs, half, other):
    query_grad, key_part, value_part, held, sems = refs[-5:]
    tokens = query.shape[0]
    both = one_doc(docs)
    enter32 = column(docs, True, F32)
    base = (1 - my_core() if other else my_core()) * half
    copies = []
    for heads in batches(half, 2):
        results = []
        for head in heads:
            cols, full = pl.ds(head * 128, 128), wide(base, head)
            q, k, v = query[:, full], key[:, full], value[:, full]
            if other:
                a = refs[0][pl.ds(0, tokens), cols].astype(BF16)
                state = refs[0][pl.ds(tokens, 128), cols].astype(BF16)
            else:
                a, state = refs[0][:, cols], refs[1][cols, :]
            pair = lower(dot(a, v, 1, 1), both)
            cross = enter32 * dot(a, state, 1, 1)
            results.append(
                (
                    (cross + times_lower(pair, k)).astype(BF16),
                    times_higher(higher(dot(v, a, 1, 1), both), q),
                    times_higher(higher(dot(k, q, 1, 1), both), a),
                )
            )
        for head, (query_part, key_term, value_term) in zip(heads, results):
            cols, full = pl.ds(head * 128, 128), wide(base, head)
            held[:, cols] = query_part
            copies.append(pltpu.make_async_copy(held.at[:, cols], query_grad.at[:, full], sems.at[head]))
            copies[-1].start()
            key_part[:, cols] = key_term
            value_part[:, cols] = value_term
    for copy in copies:
        copy.wait()


def finish_kernel(docs, key, value, key_part, value_part, state, *refs, half, other):
    refs, (key_held, value_held, gain_held, sems) = refs[:-4], refs[-4:]
    copies = []
    if other:
        refs, gain_grad = refs[:-1], refs[-1]
        for head in range(half):
            gain_held[pl.ds(my_core() * half + head, 1), :] = refs[0][pl.ds(head, 1), :]
            gain_held[pl.ds((1 - my_core()) * half + head, 1), :] = state[pl.ds(half * 128 + head, 1), :]
        copies.append(pltpu.make_async_copy(gain_held, gain_grad, sems.at[2, 0]))
        copies[-1].start()
    key_grad, value_grad = refs[-2:]
    leave = column(docs, False, F32)
    base = (1 - my_core() if other else my_core()) * half
    for at, heads in enumerate(batches(half, 4)):
        for head in heads:
            cols, full = pl.ds(head * 128, 128), wide(base, head)
            g = state[cols, :].astype(BF16)
            key_held[:, cols] = (key_part[:, cols] + leave * dot(value[:, full], g, 1, 1)).astype(BF16)
            value_held[:, cols] = (value_part[:, cols] + leave * dot(key[:, full], g, 1, 0)).astype(BF16)
        size = len(heads) * 128
        held = pl.ds(heads[0] * 128, size)
        full = pl.ds(pl.multiple_of((base + heads[0]) * 128, 128), size)
        copies.append(pltpu.make_async_copy(key_held.at[:, held], key_grad.at[:, full], sems.at[0, at]))
        copies.append(pltpu.make_async_copy(value_held.at[:, held], value_grad.at[:, full], sems.at[1, at]))
        copies[-2].start()
        copies[-1].start()
    for copy in copies:
        copy.wait()


def row(ref, rows, which):
    return ref[pl.ds(rows + which, 1), :]


def match(left, right):
    return jnp.where(left == right, 1.0, 0.0)


def pair_kernel(docs, own, other, *outs, half, size):
    rows = half * 128
    first = jnp.minimum(row(own, rows, FIRST), row(other, rows, FIRST))
    last = jnp.maximum(row(own, rows, LAST), row(other, rows, LAST))
    own_weight = match(row(own, rows, LAST), last)
    other_weight = match(row(other, rows, LAST), last)
    for turn, out in enumerate(outs):
        owner = lax.bitwise_xor(my_chip(), turn)
        part = pl.ds(pl.multiple_of(owner * size, size), size)
        out[pl.ds(0, size), :] = own[part, :] * own_weight + other[part, :] * other_weight
        out[pl.ds(size, IDS), :] = jnp.zeros((IDS, 128), F32)
        out[pl.ds(size + FIRST, 1), :] = first
        out[pl.ds(size + LAST, 1), :] = last


def plane_kernel(docs, c0, c1, c2, c3, out, *gain, size):
    chips = (c0, c1, c2, c3)
    last = functools.reduce(jnp.maximum, [row(c, size, LAST) for c in chips])
    out[pl.ds(0, size), :] = sum(
        c[pl.ds(0, size), :] * match(row(c, size, LAST), last) for c in chips
    )
    out[pl.ds(size, IDS), :] = jnp.zeros((IDS, 128), F32)
    out[pl.ds(size + LAST, 1), :] = last
    if gain:
        gain[0][...] = sum(c[pl.ds(size + IDS, IDS), :] for c in chips)
        out[pl.ds(size + IDS, IDS), :] = gain[0][...]


def chain_kernel(docs, c0, c1, c2, c3, *refs, size, distances, planes):
    chips = (c0, c1, c2, c3)
    backward = distances[0] < 0
    others, outs = refs[: len(distances)], refs[-CHIPS:]
    place = [lax.bitwise_xor(my_chip(), turn) for turn in range(CHIPS)]
    my_plane = lax.axis_index("ctx") // GROUP
    first = functools.reduce(jnp.minimum, [row(c, size, FIRST) for c in chips])
    coming = jnp.zeros((size, 128), F32)
    for distance, other in zip(distances, others):
        source = my_plane - distance
        inside = (source >= 0) & (source < planes)
        weight = match(row(other, size, LAST), first) * jnp.where(inside, 1.0, 0.0)
        coming = coming + other[pl.ds(0, size), :] * weight
    if backward:
        gain, sums, outs = refs[len(distances)], refs[-1], refs[-1 - CHIPS : -1]
        sums[...] = gain[...] + sum(p[pl.ds(size + IDS, IDS), :] for p in others)
    for turn, out in enumerate(outs):
        mine = row(chips[turn], size, FIRST)
        total = coming * match(mine, first)
        for other in range(CHIPS):
            if other == turn:
                continue
            ahead = place[other] > place[turn] if backward else place[other] < place[turn]
            weight = match(row(chips[other], size, LAST), mine) * jnp.where(ahead, 1.0, 0.0)
            total = total + chips[other][pl.ds(0, size), :] * weight
        out[...] = total


def spread_weights(is_first, own_first, own_last, other_first, other_last):
    ones = jnp.ones((1, 128), F32)
    joins = match(own_first, other_first)
    return (
        jnp.where(is_first, ones, joins),
        jnp.where(is_first, 0.0 * ones, match(other_last, own_first)),
        jnp.where(is_first, joins, ones),
        jnp.where(is_first, match(own_last, other_first), 0.0 * ones),
    )


def spread_kernel(docs, own, other, c0, c1, c2, c3, sums, sums_near, send, keep, total, *, half, size):
    rows = half * 128
    keep_coming, keep_other, send_coming, send_own = spread_weights(
        my_core() == 1,
        row(own, rows, FIRST),
        row(own, rows, LAST),
        row(other, rows, FIRST),
        row(other, rows, LAST),
    )
    for turn, chip in enumerate((c0, c1, c2, c3)):
        owner = lax.bitwise_xor(my_chip(), turn)
        part = pl.ds(pl.multiple_of(owner * size, size), size)
        coming = chip[pl.ds(0, size), :]
        send[part, :] = coming * send_coming + own[part, :] * send_own
        keep[part, :] = (coming * keep_coming + other[part, :] * keep_other).astype(BF16)
    total[...] = sums[...] + sums_near[...]
    send[pl.ds(rows, IDS), :] = total[...]


def shape(rows, cols, dtype):
    return jax.ShapeDtypeStruct((rows, cols), dtype)


def call(kernel, docs, args, outs, flops=0, in_specs=None, out_specs=None, aliases=None, scratch=()):
    whole = pl.BlockSpec(memory_space=pltpu.VMEM)
    in_specs = in_specs or [None] * len(args)
    out_specs = out_specs or [None] * len(outs)
    moved = sum(a.size * a.dtype.itemsize for a in list(args) + list(outs))
    return pl.pallas_call(
        kernel,
        out_shape=outs,
        grid_spec=pltpu.PrefetchScalarGridSpec(
            num_scalar_prefetch=1,
            grid=(1,),
            in_specs=[spec or whole for spec in in_specs],
            out_specs=[spec or whole for spec in out_specs],
            scratch_shapes=scratch,
        ),
        input_output_aliases=aliases or {},
        cost_estimate=pl.CostEstimate(flops=flops, bytes_accessed=moved, transcendentals=0),
        compiler_params=pltpu.CompilerParams(vmem_limit_bytes=32 * 1024 * 1024),
    )(docs, *args)


def tie(value, *after):
    return lax.optimization_barrier((value, after))[0]


def local(queries, key_rows, value_rows, out_grad, norm_gain, doc_ids, *, shards, dp):
    tokens = queries.shape[1]
    heads, width = norm_gain.shape
    half = heads // 2
    rows, cols = half * width, heads * width
    size = rows // CHIPS
    query, key, value, grad = (
        a.reshape(tokens, cols) for a in (queries, key_rows, value_rows, out_grad)
    )
    planes = shards // GROUP
    any_place = pl.BlockSpec(memory_space=pl.ANY)

    def swap(value):
        return lax.ppermute(value, "ctx", [(i, i ^ 1) for i in range(shards)])

    def to_chips(values):
        return [values[0]] + [
            lax.ppermute(values[turn], "ctx", [(i, i ^ (2 * turn)) for i in range(shards)])
            for turn in (1, 2, 3)
        ]

    def around(value, distance):
        pairs = [(i, (i + distance * GROUP) % shards) for i in range(shards)]
        return lax.ppermute(value, "ctx", pairs)

    payload = shape(rows + IDS, width, F32)

    def chain(sent, backward, beside_up, beside_planes, beside_down):
        chunks = tie(to_chips(sent), beside_up(sent))
        plane, *gain = call(
            functools.partial(plane_kernel, size=size),
            doc_ids,
            chunks,
            [shape(size + (2 * IDS if backward else IDS), width, F32)]
            + ([shape(IDS, width, F32)] if backward else []),
        )
        distances = (-1, -2) if backward else (1, 2)
        others = [around(plane, distance) for distance in distances]
        others = tie(others, beside_planes(plane))
        sent = call(
            functools.partial(chain_kernel, size=size, distances=distances, planes=planes),
            doc_ids,
            [*chunks, *others, *gain],
            [shape(size, width, F32)] * CHIPS + ([shape(IDS, width, F32)] if backward else []),
        )
        return tie(to_chips(sent[:CHIPS]), beside_down(sent, *gain))

    def within(other, sources, into):
        spare = [] if into is None else [into]
        at = 3 + len(sources)
        return call(
            functools.partial(within_kernel, half=half, other=other),
            doc_ids,
            [query, key, value, *sources, *spare],
            [shape(tokens, cols, BF16), shape(tokens, rows, F32), shape(tokens, rows, F32)],
            flops=2 * half * tokens * width * (6 * tokens + width),
            in_specs=[None] * at + [any_place] * len(spare),
            out_specs=[any_place] + [None] * 2,
            aliases={1 + at: 0} if spare else None,
            scratch=[pltpu.VMEM((tokens, rows), BF16), pltpu.SemaphoreType.DMA((half,))],
        )

    def finish(other, parts, state, sums, into):
        return call(
            functools.partial(finish_kernel, half=half, other=other),
            doc_ids,
            [key, value, *parts, state, *sums, *into],
            [shape(tokens, cols, BF16)] * 2 + [shape(heads, width, F32)] * len(sums),
            flops=2 * half * tokens * width * 2 * width,
            in_specs=[None] * (5 + len(sums)) + [any_place] * len(into),
            out_specs=[any_place] * (2 + len(sums)),
            aliases={7: 0, 8: 1} if into else None,
            scratch=[
                pltpu.VMEM((tokens, rows), BF16),
                pltpu.VMEM((tokens, rows), BF16),
                pltpu.VMEM((heads, width), F32),
                pltpu.SemaphoreType.DMA((3, half)),
            ],
        )

    hbm = pl.BlockSpec(memory_space=pltpu.HBM)
    vmem = pl.BlockSpec(memory_space=pltpu.VMEM)
    half_shape = shape(tokens, rows, BF16)
    states, key_own, value_own = pl.pallas_call(
        functools.partial(first_kernel, half=half),
        out_shape=[payload, half_shape, half_shape],
        in_specs=[hbm] * 3,
        out_specs=[vmem] * 3,
        scratch_shapes=[
            pltpu.SMEM(doc_ids.shape, jnp.int32),
            pltpu.VMEM(half_shape.shape, BF16),
            pltpu.VMEM(half_shape.shape, BF16),
            pltpu.SemaphoreType.DMA((5,)),
        ],
        cost_estimate=pl.CostEstimate(
            flops=2 * half * tokens * width * width, bytes_accessed=4 * tokens * rows * 2, transcendentals=0
        ),
        compiler_params=pltpu.CompilerParams(vmem_limit_bytes=32 * 1024 * 1024),
    )(*(pltpu.with_memory_space_constraint(x, pltpu.HBM) for x in (doc_ids, key, value)))
    received = swap(states)
    query, key, value, grad, doc_ids = tie((query, key, value, grad, doc_ids), states)
    (own,) = call(
        functools.partial(second_kernel, half=half),
        doc_ids,
        [key_own, value_own],
        [payload],
        flops=2 * half * tokens * width * width,
    )
    sent = call(
        functools.partial(pair_kernel, half=half, size=size),
        doc_ids,
        [own, received],
        [shape(size + IDS, width, F32)] * CHIPS,
    )

    kept = {}

    def intra(sent):
        kept["inside"], kept["message"] = call(
            functools.partial(intra_kernel, half=half),
            doc_ids,
            [tie(query, sent), key, value, grad],
            [shape(tokens, rows, F32), shape(3 * tokens, rows, F32)],
            flops=2 * heads * tokens * width * 2 * tokens,
        )
        return kept["inside"]

    def forward_message(plane):
        kept["message"] = swap(tie(kept["message"], plane))
        return []

    coming = chain(sent, False, intra, forward_message, lambda sent: [])
    *sent, back, back_other, attn, reply, state = call(
        functools.partial(middle_kernel, half=half, size=size),
        doc_ids,
        [own, received, *coming, query, grad, kept["inside"], kept["message"], norm_gain],
        [shape(size + 2 * IDS, width, F32)] * CHIPS
        + [payload, payload]
        + [shape(tokens, rows, BF16), shape(tokens + width, rows, F32), shape(rows, width, BF16)],
        flops=2 * heads * tokens * width * 2 * width,
    )

    def beside_up(sent):
        kept["first"] = within(False, [tie(attn, sent), state], None)
        return kept["first"]

    def beside_planes(plane):
        kept["reply"] = swap(tie(reply, plane))
        return []

    def beside_down(sent, gain):
        kept["sums"] = [sent[-1], around(tie(gain, sent), 1)]
        kept["second"] = within(True, [tie(kept["reply"], sent)], kept["first"][0])
        return kept["second"]

    coming = chain(sent, True, beside_up, beside_planes, beside_down)
    send, out_state, total = call(
        functools.partial(spread_kernel, half=half, size=size),
        doc_ids,
        [back, back_other, *coming, *kept["sums"]],
        [shape(rows + IDS, width, F32), shape(rows, width, BF16), shape(IDS, width, F32)],
    )
    out_received = swap(send)
    grads = finish(False, kept["first"][1:], out_state, [], [])
    out_received, grads = lax.optimization_barrier((out_received, grads))
    query_grad, *parts = kept["second"]
    key_grad, value_grad, gain_grad = finish(True, parts, out_received, [total], grads)
    if dp > 1:
        gain_grad = lax.psum_scatter(gain_grad, "dp", scatter_dimension=1, tiled=True)
    flat = (1, tokens, cols)
    return (query_grad.reshape(flat), key_grad.reshape(flat), value_grad.reshape(flat), gain_grad)


def solution(mesh):
    in_specs = (
        P("dp", "ctx", "tp"),
        P("dp", "ctx", "tp"),
        P("dp", "ctx", "tp"),
        P("dp", "ctx", "tp"),
        P("tp", None),
        P("dp", "ctx"),
    )
    out_specs = (P("dp", "ctx", "tp"), P("dp", "ctx", "tp"), P("dp", "ctx", "tp"), P("tp", "dp"))
    body = functools.partial(local, shards=mesh.shape["ctx"], dp=mesh.shape["dp"])
    return jax.shard_map(body, mesh=mesh, in_specs=in_specs, out_specs=out_specs, check_vma=False)
```

```python
import functools

import jax
import jax.numpy as jnp
from jax import lax
from jax.experimental import pallas as pl
from jax.experimental.pallas import tpu as pltpu
from jax.sharding import PartitionSpec as P

BLK = 128
EPSILON = 1e-06
CHIPS = 4
TURNS = (0, 3, 1, 2)
GROUP = 2 * CHIPS
IDS = 8
FIRST, LAST = 0, 1
F32, BF16 = jnp.float32, jnp.bfloat16


def dot(left, right, left_dim, right_dim):
    return lax.dot_general(
        left, right, (((left_dim,), (right_dim,)), ((), ())), preferred_element_type=F32
    )


def my_core():
    return lax.axis_index("ctx") % 2


def my_chip():
    return (lax.axis_index("ctx") // 2) % CHIPS


def one_doc(docs):
    return jnp.where(docs[0, 0] == docs[0, 1], 1.0, 0.0)


def column(docs, first_block, dtype):
    rows = lax.broadcasted_iota(jnp.int32, (2 * BLK, 1), 0)
    own = (rows < BLK) if first_block else (rows >= BLK)
    return jnp.where(own, 1.0, one_doc(docs)).astype(dtype)


def lower(table, both):
    rows = lax.broadcasted_iota(jnp.int32, (BLK, BLK), 0)
    cols = lax.broadcasted_iota(jnp.int32, (BLK, BLK), 1)
    keep = rows >= cols
    upper = jnp.where(keep, table[:BLK, :BLK], 0.0).astype(BF16)
    below = (table[BLK:, :BLK] * both).astype(BF16)
    right = jnp.where(keep, table[BLK:, BLK:], 0.0).astype(BF16)
    return upper, jnp.concatenate([below, right], 1)


def higher(table, both):
    rows = lax.broadcasted_iota(jnp.int32, (BLK, BLK), 0)
    cols = lax.broadcasted_iota(jnp.int32, (BLK, BLK), 1)
    keep = rows <= cols
    left = jnp.where(keep, table[:BLK, :BLK], 0.0).astype(BF16)
    above = (table[:BLK, BLK:] * both).astype(BF16)
    below = jnp.where(keep, table[BLK:, BLK:], 0.0).astype(BF16)
    return jnp.concatenate([left, above], 1), below


def times_lower(masked, values):
    upper, below = masked
    return jnp.concatenate([dot(upper, values[:BLK], 1, 0), dot(below, values, 1, 0)], 0)


def times_higher(masked, values):
    above, lower_right = masked
    return jnp.concatenate([dot(above, values, 1, 0), dot(lower_right, values[BLK:], 1, 0)], 0)


def write_ids(docs, out, rows, backward):
    first, last = docs[0, 0].astype(F32), docs[0, 1].astype(F32)
    if backward:
        first, last = -last, -first
    out[pl.ds(rows, IDS), :] = jnp.zeros((IDS, 128), F32)
    out[pl.ds(rows + FIRST, 1), :] = jnp.full((1, 128), first, F32)
    out[pl.ds(rows + LAST, 1), :] = jnp.full((1, 128), last, F32)


def wide(base, head):
    return pl.ds(pl.multiple_of((base + head) * 128, 128), 128)


def batches(total, most):
    most = most if total % most == 0 else 1
    return [range(start, start + most) for start in range(0, total, most)]


def element(docs, key, value, out, first_col, half):
    weight = column(docs, False, BF16)
    write_ids(docs, out, half * 128, False)
    for heads in batches(half, 4):
        columns = [wide(first_col, head) for head in heads]
        states = [dot(key[:, at] * weight, value[:, at], 0, 0) for at in columns]
        for head, state in zip(heads, states):
            out[pl.ds(head * 128, 128), :] = state


def first_kernel(docs, key, value, out, key_own, value_own, docs_held, key_held, value_held, sems, *, half):
    core, rows = my_core(), half * 128
    far = pl.ds(pl.multiple_of((1 - core) * rows, rows), rows)
    own = pl.ds(pl.multiple_of(core * rows, rows), rows)
    copies = [
        pltpu.make_async_copy(docs, docs_held, sems.at[0]),
        pltpu.make_async_copy(key.at[:, far], key_held, sems.at[1]),
        pltpu.make_async_copy(value.at[:, far], value_held, sems.at[2]),
        pltpu.make_async_copy(key.at[:, own], key_own, sems.at[3]),
        pltpu.make_async_copy(value.at[:, own], value_own, sems.at[4]),
    ]
    for copy in copies:
        copy.start()
    for copy in copies[:3]:
        copy.wait()
    element(docs_held, key_held, value_held, out, 0, half)
    for copy in copies[3:]:
        copy.wait()


def second_kernel(docs, key, value, out, *, half):
    element(docs, key, value, out, 0, half)


def intra_kernel(docs, query, key, value, grad, own, message, *, half):
    both = one_doc(docs)
    tokens = query.shape[0]
    for other in (True, False):
        base = (1 - my_core() if other else my_core()) * half
        for heads in batches(half, 2):
            results = []
            for head in heads:
                full = wide(base, head)
                q = query[:, full]
                scores = lower(dot(q, key[:, full], 1, 1), both)
                part = times_lower(scores, value[:, full])
                results.append((q.astype(F32), grad[:, full].astype(F32), part) if other else (part,))
            for head, parts in zip(heads, results):
                cols = pl.ds(head * 128, 128)
                if other:
                    for at, part in enumerate(parts):
                        message[pl.ds(at * tokens, tokens), cols] = part
                else:
                    own[:, cols] = parts[0]


def attend(q, g, intra, state, gain, joined):
    inter = dot(q, state, 1, 0)
    attended = intra + jnp.concatenate([inter[:BLK], inter[BLK:] * joined], 0)
    inv_rms = lax.rsqrt(jnp.mean(attended * attended, -1, keepdims=True) + EPSILON)
    scaled = g * gain
    normed = attended * inv_rms
    terms = jnp.sum(g * normed, 0, keepdims=True)
    mean = jnp.mean(scaled * normed, -1, keepdims=True)
    attn = (inv_rms * (scaled - normed * mean)).astype(BF16)
    back = dot(q[:BLK], attn[:BLK], 0, 0) + dot(q[BLK:], attn[BLK:], 0, 0) * joined
    return attn, back, terms


def middle_kernel(
    docs, own, other, c0, c1, c2, c3, query, grad, intra, message, gain,
    up0, up1, up2, up3, back_own, back_other, attn_own, reply, state_own, *, half, size,
):
    rows, tokens, chunk = half * 128, query.shape[0], size // 128
    base = my_core() * half
    is_first = my_core() == 0
    own_first, own_last = row(own, rows, FIRST), row(own, rows, LAST)
    other_first, other_last = row(other, rows, FIRST), row(other, rows, LAST)
    keep_coming, keep_other, send_coming, send_own = spread_weights(
        is_first, own_first, own_last, other_first, other_last
    )
    own_joined, other_joined = match(own_first, own_last), match(other_first, other_last)
    for back, first, last in ((back_own, own_first, own_last), (back_other, other_first, other_last)):
        back[pl.ds(rows, IDS), :] = jnp.zeros((IDS, 128), F32)
        back[pl.ds(rows + FIRST, 1), :] = -last
        back[pl.ds(rows + LAST, 1), :] = -first
    first = jnp.minimum(own_first, other_first)
    last = jnp.maximum(own_last, other_last)
    own_weight, other_weight = match(own_first, first), match(other_first, first)
    ups = (up0, up1, up2, up3)
    for up in ups:
        up[pl.ds(size, 2 * IDS), :] = jnp.zeros((2 * IDS, 128), F32)
        up[pl.ds(size + FIRST, 1), :] = -last
        up[pl.ds(size + LAST, 1), :] = -first
    for turn, chip in enumerate((c0, c1, c2, c3)):
        results = []
        for step in range(chunk):
            head = lax.bitwise_xor(my_chip(), TURNS[turn]) * chunk + step
            cols, full = wide(0, head), wide(base, head)
            coming = chip[pl.ds(step * 128, 128), :]
            state = (coming * keep_coming + other[cols, :] * keep_other).astype(BF16)
            state_other = coming * send_coming + own[cols, :] * send_own
            weights = gain[pl.ds(base + head, 1), :]
            near = attend(
                query[:, full], grad[:, full].astype(F32), intra[:, cols], state, weights, own_joined
            )
            far = attend(
                message[pl.ds(0, tokens), cols].astype(BF16),
                message[pl.ds(tokens, tokens), cols],
                message[pl.ds(2 * tokens, tokens), cols],
                state_other.astype(BF16),
                weights,
                other_joined,
            )
            results.append((head, cols, state, state_other, near, far))
        for step, (head, cols, state, state_other, near, far) in enumerate(results):
            attn, back, terms = near
            attn_far, back_far, terms_far = far
            state_own[cols, :] = state
            reply[pl.ds(tokens, 128), cols] = state_other
            attn_own[:, cols] = attn
            back_own[cols, :] = back
            reply[pl.ds(0, tokens), cols] = attn_far.astype(F32)
            back_other[cols, :] = back_far
            ups[turn][pl.ds(step * 128, 128), :] = back * own_weight + back_far * other_weight
            for up in ups:
                up[pl.ds(size + IDS + head, 1), :] = terms + terms_far


def within_kernel(docs, query, key, value, *refs, half, other):
    query_grad, key_part, value_part, held, sems = refs[-5:]
    tokens = query.shape[0]
    both = one_doc(docs)
    enter32 = column(docs, True, F32)
    base = (1 - my_core() if other else my_core()) * half
    copies = []
    for heads in batches(half, 2):
        results = []
        for head in heads:
            cols, full = pl.ds(head * 128, 128), wide(base, head)
            q, k, v = query[:, full], key[:, full], value[:, full]
            if other:
                a = refs[0][pl.ds(0, tokens), cols].astype(BF16)
                state = refs[0][pl.ds(tokens, 128), cols].astype(BF16)
            else:
                a, state = refs[0][:, cols], refs[1][cols, :]
            pair = lower(dot(a, v, 1, 1), both)
            cross = enter32 * dot(a, state, 1, 1)
            results.append(
                (
                    (cross + times_lower(pair, k)).astype(BF16),
                    times_higher(higher(dot(v, a, 1, 1), both), q),
                    times_higher(higher(dot(k, q, 1, 1), both), a),
                )
            )
        for head, (query_part, key_term, value_term) in zip(heads, results):
            cols, full = pl.ds(head * 128, 128), wide(base, head)
            held[:, cols] = query_part
            copies.append(pltpu.make_async_copy(held.at[:, cols], query_grad.at[:, full], sems.at[head]))
            copies[-1].start()
            key_part[:, cols] = key_term
            value_part[:, cols] = value_term
    for copy in copies:
        copy.wait()


def finish_kernel(docs, key, value, key_part, value_part, state, *refs, half, other):
    refs, (key_held, value_held, gain_held, sems) = refs[:-4], refs[-4:]
    copies = []
    if other:
        refs, gain_grad = refs[:-1], refs[-1]
        for head in range(half):
            gain_held[pl.ds(my_core() * half + head, 1), :] = refs[0][pl.ds(head, 1), :]
            gain_held[pl.ds((1 - my_core()) * half + head, 1), :] = state[pl.ds(half * 128 + head, 1), :]
        copies.append(pltpu.make_async_copy(gain_held, gain_grad, sems.at[2, 0]))
        copies[-1].start()
    key_grad, value_grad = refs[-2:]
    leave = column(docs, False, F32)
    base = (1 - my_core() if other else my_core()) * half
    for at, heads in enumerate(batches(half, 4)):
        for head in heads:
            cols, full = pl.ds(head * 128, 128), wide(base, head)
            g = state[cols, :].astype(BF16)
            key_held[:, cols] = (key_part[:, cols] + leave * dot(value[:, full], g, 1, 1)).astype(BF16)
            value_held[:, cols] = (value_part[:, cols] + leave * dot(key[:, full], g, 1, 0)).astype(BF16)
        size = len(heads) * 128
        held = pl.ds(heads[0] * 128, size)
        full = pl.ds(pl.multiple_of((base + heads[0]) * 128, 128), size)
        copies.append(pltpu.make_async_copy(key_held.at[:, held], key_grad.at[:, full], sems.at[0, at]))
        copies.append(pltpu.make_async_copy(value_held.at[:, held], value_grad.at[:, full], sems.at[1, at]))
        copies[-2].start()
        copies[-1].start()
    for copy in copies:
        copy.wait()


def row(ref, rows, which):
    return ref[pl.ds(rows + which, 1), :]


def match(left, right):
    return jnp.where(left == right, 1.0, 0.0)


def pair_kernel(docs, own, other, *outs, half, size):
    rows = half * 128
    first = jnp.minimum(row(own, rows, FIRST), row(other, rows, FIRST))
    last = jnp.maximum(row(own, rows, LAST), row(other, rows, LAST))
    own_weight = match(row(own, rows, LAST), last)
    other_weight = match(row(other, rows, LAST), last)
    for turn, out in enumerate(outs):
        owner = lax.bitwise_xor(my_chip(), TURNS[turn])
        part = pl.ds(pl.multiple_of(owner * size, size), size)
        out[pl.ds(0, size), :] = own[part, :] * own_weight + other[part, :] * other_weight
        out[pl.ds(size, IDS), :] = jnp.zeros((IDS, 128), F32)
        out[pl.ds(size + FIRST, 1), :] = first
        out[pl.ds(size + LAST, 1), :] = last


def plane_kernel(docs, c0, c1, c2, c3, out, *gain, size):
    chips = (c0, c1, c2, c3)
    last = functools.reduce(jnp.maximum, [row(c, size, LAST) for c in chips])
    out[pl.ds(0, size), :] = sum(
        c[pl.ds(0, size), :] * match(row(c, size, LAST), last) for c in chips
    )
    out[pl.ds(size, IDS), :] = jnp.zeros((IDS, 128), F32)
    out[pl.ds(size + LAST, 1), :] = last
    if gain:
        gain[0][...] = sum(c[pl.ds(size + IDS, IDS), :] for c in chips)
        out[pl.ds(size + IDS, IDS), :] = gain[0][...]


def chain_kernel(docs, c0, c1, c2, c3, *refs, size, distances, planes):
    chips = (c0, c1, c2, c3)
    backward = distances[0] < 0
    others, outs = refs[: len(distances)], refs[-CHIPS:]
    place = [lax.bitwise_xor(my_chip(), TURNS[turn]) for turn in range(CHIPS)]
    my_plane = lax.axis_index("ctx") // GROUP
    first = functools.reduce(jnp.minimum, [row(c, size, FIRST) for c in chips])
    coming = jnp.zeros((size, 128), F32)
    for distance, other in zip(distances, others):
        source = my_plane - distance
        inside = (source >= 0) & (source < planes)
        weight = match(row(other, size, LAST), first) * jnp.where(inside, 1.0, 0.0)
        coming = coming + other[pl.ds(0, size), :] * weight
    if backward:
        gain, sums, outs = refs[len(distances)], refs[-1], refs[-1 - CHIPS : -1]
        sums[...] = gain[...] + sum(p[pl.ds(size + IDS, IDS), :] for p in others)
    for turn, out in enumerate(outs):
        mine = row(chips[turn], size, FIRST)
        total = coming * match(mine, first)
        for other in range(CHIPS):
            if other == turn:
                continue
            ahead = place[other] > place[turn] if backward else place[other] < place[turn]
            weight = match(row(chips[other], size, LAST), mine) * jnp.where(ahead, 1.0, 0.0)
            total = total + chips[other][pl.ds(0, size), :] * weight
        out[...] = total


def spread_weights(is_first, own_first, own_last, other_first, other_last):
    ones = jnp.ones((1, 128), F32)
    joins = match(own_first, other_first)
    return (
        jnp.where(is_first, ones, joins),
        jnp.where(is_first, 0.0 * ones, match(other_last, own_first)),
        jnp.where(is_first, joins, ones),
        jnp.where(is_first, match(own_last, other_first), 0.0 * ones),
    )


def spread_kernel(docs, own, other, c0, c1, c2, c3, sums, sums_near, send, keep, total, *, half, size):
    rows = half * 128
    keep_coming, keep_other, send_coming, send_own = spread_weights(
        my_core() == 1,
        row(own, rows, FIRST),
        row(own, rows, LAST),
        row(other, rows, FIRST),
        row(other, rows, LAST),
    )
    for turn, chip in enumerate((c0, c1, c2, c3)):
        owner = lax.bitwise_xor(my_chip(), TURNS[turn])
        part = pl.ds(pl.multiple_of(owner * size, size), size)
        coming = chip[pl.ds(0, size), :]
        send[part, :] = coming * send_coming + own[part, :] * send_own
        keep[part, :] = (coming * keep_coming + other[part, :] * keep_other).astype(BF16)
    total[...] = sums[...] + sums_near[...]
    send[pl.ds(rows, IDS), :] = total[...]


def shape(rows, cols, dtype):
    return jax.ShapeDtypeStruct((rows, cols), dtype)


def call(kernel, docs, args, outs, flops=0, in_specs=None, out_specs=None, aliases=None, scratch=()):
    whole = pl.BlockSpec(memory_space=pltpu.VMEM)
    in_specs = in_specs or [None] * len(args)
    out_specs = out_specs or [None] * len(outs)
    moved = sum(a.size * a.dtype.itemsize for a in list(args) + list(outs))
    return pl.pallas_call(
        kernel,
        out_shape=outs,
        grid_spec=pltpu.PrefetchScalarGridSpec(
            num_scalar_prefetch=1,
            grid=(1,),
            in_specs=[spec or whole for spec in in_specs],
            out_specs=[spec or whole for spec in out_specs],
            scratch_shapes=scratch,
        ),
        input_output_aliases=aliases or {},
        cost_estimate=pl.CostEstimate(flops=flops, bytes_accessed=moved, transcendentals=0),
        compiler_params=pltpu.CompilerParams(vmem_limit_bytes=32 * 1024 * 1024),
    )(docs, *args)


def tie(value, *after):
    return lax.optimization_barrier((value, after))[0]


def local(queries, key_rows, value_rows, out_grad, norm_gain, doc_ids, *, shards, dp):
    tokens = queries.shape[1]
    heads, width = norm_gain.shape
    half = heads // 2
    rows, cols = half * width, heads * width
    size = rows // CHIPS
    query, key, value, grad = (
        a.reshape(tokens, cols) for a in (queries, key_rows, value_rows, out_grad)
    )
    planes = shards // GROUP
    any_place = pl.BlockSpec(memory_space=pl.ANY)

    def swap(value):
        return lax.ppermute(value, "ctx", [(i, i ^ 1) for i in range(shards)])

    def to_chips(values):
        return [values[0]] + [
            lax.ppermute(values[turn], "ctx", [(i, i ^ (2 * TURNS[turn])) for i in range(shards)])
            for turn in (1, 2, 3)
        ]

    def around(value, distance):
        pairs = [(i, (i + distance * GROUP) % shards) for i in range(shards)]
        return lax.ppermute(value, "ctx", pairs)

    payload = shape(rows + IDS, width, F32)

    def chain(sent, backward, beside_up, beside_planes, beside_down):
        chunks = tie(to_chips(sent), beside_up(sent))
        plane, *gain = call(
            functools.partial(plane_kernel, size=size),
            doc_ids,
            chunks,
            [shape(size + (2 * IDS if backward else IDS), width, F32)]
            + ([shape(IDS, width, F32)] if backward else []),
        )
        distances = (-1, -2) if backward else (1, 2)
        others = [around(plane, distance) for distance in distances]
        others = tie(others, beside_planes(plane))
        sent = call(
            functools.partial(chain_kernel, size=size, distances=distances, planes=planes),
            doc_ids,
            [*chunks, *others, *gain],
            [shape(size, width, F32)] * CHIPS + ([shape(IDS, width, F32)] if backward else []),
        )
        return tie(to_chips(sent[:CHIPS]), beside_down(sent, *gain))

    def within(other, sources, into):
        spare = [] if into is None else [into]
        at = 3 + len(sources)
        return call(
            functools.partial(within_kernel, half=half, other=other),
            doc_ids,
            [query, key, value, *sources, *spare],
            [shape(tokens, cols, BF16), shape(tokens, rows, F32), shape(tokens, rows, F32)],
            flops=2 * half * tokens * width * (6 * tokens + width),
            in_specs=[None] * at + [any_place] * len(spare),
            out_specs=[any_place] + [None] * 2,
            aliases={1 + at: 0} if spare else None,
            scratch=[pltpu.VMEM((tokens, rows), BF16), pltpu.SemaphoreType.DMA((half,))],
        )

    def finish(other, parts, state, sums, into):
        return call(
            functools.partial(finish_kernel, half=half, other=other),
            doc_ids,
            [key, value, *parts, state, *sums, *into],
            [shape(tokens, cols, BF16)] * 2 + [shape(heads, width, F32)] * len(sums),
            flops=2 * half * tokens * width * 2 * width,
            in_specs=[None] * (5 + len(sums)) + [any_place] * len(into),
            out_specs=[any_place] * (2 + len(sums)),
            aliases={7: 0, 8: 1} if into else None,
            scratch=[
                pltpu.VMEM((tokens, rows), BF16),
                pltpu.VMEM((tokens, rows), BF16),
                pltpu.VMEM((heads, width), F32),
                pltpu.SemaphoreType.DMA((3, half)),
            ],
        )

    hbm = pl.BlockSpec(memory_space=pltpu.HBM)
    vmem = pl.BlockSpec(memory_space=pltpu.VMEM)
    half_shape = shape(tokens, rows, BF16)
    states, key_own, value_own = pl.pallas_call(
        functools.partial(first_kernel, half=half),
        out_shape=[payload, half_shape, half_shape],
        in_specs=[hbm] * 3,
        out_specs=[vmem] * 3,
        scratch_shapes=[
            pltpu.SMEM(doc_ids.shape, jnp.int32),
            pltpu.VMEM(half_shape.shape, BF16),
            pltpu.VMEM(half_shape.shape, BF16),
            pltpu.SemaphoreType.DMA((5,)),
        ],
        cost_estimate=pl.CostEstimate(
            flops=2 * half * tokens * width * width, bytes_accessed=4 * tokens * rows * 2, transcendentals=0
        ),
        compiler_params=pltpu.CompilerParams(vmem_limit_bytes=32 * 1024 * 1024),
    )(*(pltpu.with_memory_space_constraint(x, pltpu.HBM) for x in (doc_ids, key, value)))
    received = swap(states)
    query, key, value, grad, doc_ids = tie((query, key, value, grad, doc_ids), states)
    (own,) = call(
        functools.partial(second_kernel, half=half),
        doc_ids,
        [key_own, value_own],
        [payload],
        flops=2 * half * tokens * width * width,
    )
    sent = call(
        functools.partial(pair_kernel, half=half, size=size),
        doc_ids,
        [own, received],
        [shape(size + IDS, width, F32)] * CHIPS,
    )

    kept = {}

    def intra(sent):
        kept["inside"], kept["message"] = call(
            functools.partial(intra_kernel, half=half),
            doc_ids,
            [tie(query, sent), key, value, grad],
            [shape(tokens, rows, F32), shape(3 * tokens, rows, F32)],
            flops=2 * heads * tokens * width * 2 * tokens,
        )
        return kept["inside"]

    def forward_message(plane):
        kept["message"] = swap(tie(kept["message"], plane))
        return []

    coming = chain(sent, False, intra, forward_message, lambda sent: [])
    *sent, back, back_other, attn, reply, state = call(
        functools.partial(middle_kernel, half=half, size=size),
        doc_ids,
        [own, received, *coming, query, grad, kept["inside"], kept["message"], norm_gain],
        [shape(size + 2 * IDS, width, F32)] * CHIPS
        + [payload, payload]
        + [shape(tokens, rows, BF16), shape(tokens + width, rows, F32), shape(rows, width, BF16)],
        flops=2 * heads * tokens * width * 2 * width,
    )

    def beside_up(sent):
        kept["first"] = within(False, [tie(attn, sent), state], None)
        return kept["first"]

    def beside_planes(plane):
        kept["reply"] = swap(tie(reply, plane))
        return []

    def beside_down(sent, gain):
        kept["sums"] = [sent[-1], around(tie(gain, sent), 1)]
        kept["second"] = within(True, [tie(kept["reply"], sent)], kept["first"][0])
        return kept["second"]

    coming = chain(sent, True, beside_up, beside_planes, beside_down)
    send, out_state, total = call(
        functools.partial(spread_kernel, half=half, size=size),
        doc_ids,
        [back, back_other, *coming, *kept["sums"]],
        [shape(rows + IDS, width, F32), shape(rows, width, BF16), shape(IDS, width, F32)],
    )
    out_received = swap(send)
    grads = finish(False, kept["first"][1:], out_state, [], [])
    out_received, grads = lax.optimization_barrier((out_received, grads))
    query_grad, *parts = kept["second"]
    key_grad, value_grad, gain_grad = finish(True, parts, out_received, [total], grads)
    if dp > 1:
        gain_grad = lax.psum_scatter(gain_grad, "dp", scatter_dimension=1, tiled=True)
    flat = (1, tokens, cols)
    return (query_grad.reshape(flat), key_grad.reshape(flat), value_grad.reshape(flat), gain_grad)


def solution(mesh):
    in_specs = (
        P("dp", "ctx", "tp"),
        P("dp", "ctx", "tp"),
        P("dp", "ctx", "tp"),
        P("dp", "ctx", "tp"),
        P("tp", None),
        P("dp", "ctx"),
    )
    out_specs = (P("dp", "ctx", "tp"), P("dp", "ctx", "tp"), P("dp", "ctx", "tp"), P("tp", "dp"))
    body = functools.partial(local, shards=mesh.shape["ctx"], dp=mesh.shape["dp"])
    return jax.shard_map(body, mesh=mesh, in_specs=in_specs, out_specs=out_specs, check_vma=False)
```

```python
import functools

import jax
import jax.numpy as jnp
from jax import lax
from jax.experimental import pallas as pl
from jax.experimental.pallas import tpu as pltpu
from jax.sharding import PartitionSpec as P

BLK = 128
EPSILON = 1e-06
CHIPS = 4
GROUP = 2 * CHIPS
IDS = 8
FIRST, LAST = 0, 1
F32, BF16 = jnp.float32, jnp.bfloat16


def dot(left, right, left_dim, right_dim):
    return lax.dot_general(
        left, right, (((left_dim,), (right_dim,)), ((), ())), preferred_element_type=F32
    )


def my_core():
    return lax.axis_index("ctx") % 2


def my_chip():
    return (lax.axis_index("ctx") // 2) % CHIPS


def one_doc(docs):
    return jnp.where(docs[0, 0] == docs[0, 1], 1.0, 0.0)


def column(docs, first_block, dtype):
    rows = lax.broadcasted_iota(jnp.int32, (2 * BLK, 1), 0)
    own = (rows < BLK) if first_block else (rows >= BLK)
    return jnp.where(own, 1.0, one_doc(docs)).astype(dtype)


def lower(table, both):
    rows = lax.broadcasted_iota(jnp.int32, (BLK, BLK), 0)
    cols = lax.broadcasted_iota(jnp.int32, (BLK, BLK), 1)
    keep = rows >= cols
    upper = jnp.where(keep, table[:BLK, :BLK], 0.0).astype(BF16)
    below = (table[BLK:, :BLK] * both).astype(BF16)
    right = jnp.where(keep, table[BLK:, BLK:], 0.0).astype(BF16)
    return upper, jnp.concatenate([below, right], 1)


def higher(table, both):
    rows = lax.broadcasted_iota(jnp.int32, (BLK, BLK), 0)
    cols = lax.broadcasted_iota(jnp.int32, (BLK, BLK), 1)
    keep = rows <= cols
    left = jnp.where(keep, table[:BLK, :BLK], 0.0).astype(BF16)
    above = (table[:BLK, BLK:] * both).astype(BF16)
    below = jnp.where(keep, table[BLK:, BLK:], 0.0).astype(BF16)
    return jnp.concatenate([left, above], 1), below


def times_lower(masked, values):
    upper, below = masked
    return jnp.concatenate([dot(upper, values[:BLK], 1, 0), dot(below, values, 1, 0)], 0)


def times_higher(masked, values):
    above, lower_right = masked
    return jnp.concatenate([dot(above, values, 1, 0), dot(lower_right, values[BLK:], 1, 0)], 0)


def write_ids(docs, out, rows, backward):
    first, last = docs[0, 0].astype(F32), docs[0, 1].astype(F32)
    if backward:
        first, last = -last, -first
    out[pl.ds(rows, IDS), :] = jnp.zeros((IDS, 128), F32)
    out[pl.ds(rows + FIRST, 1), :] = jnp.full((1, 128), first, F32)
    out[pl.ds(rows + LAST, 1), :] = jnp.full((1, 128), last, F32)


def wide(base, head):
    return pl.ds(pl.multiple_of((base + head) * 128, 128), 128)


def batches(total, most):
    most = most if total % most == 0 else 1
    return [range(start, start + most) for start in range(0, total, most)]


def element(docs, key, value, out, first_col, half):
    weight = column(docs, False, BF16)
    write_ids(docs, out, half * 128, False)
    for heads in batches(half, 4):
        columns = [wide(first_col, head) for head in heads]
        states = [dot(key[:, at] * weight, value[:, at], 0, 0) for at in columns]
        for head, state in zip(heads, states):
            out[pl.ds(head * 128, 128), :] = state


def first_kernel(docs, key, value, out, key_own, value_own, docs_held, key_held, value_held, sems, *, half):
    core, rows = my_core(), half * 128
    far = pl.ds(pl.multiple_of((1 - core) * rows, rows), rows)
    own = pl.ds(pl.multiple_of(core * rows, rows), rows)
    copies = [
        pltpu.make_async_copy(docs, docs_held, sems.at[0]),
        pltpu.make_async_copy(key.at[:, far], key_held, sems.at[1]),
        pltpu.make_async_copy(value.at[:, far], value_held, sems.at[2]),
        pltpu.make_async_copy(key.at[:, own], key_own, sems.at[3]),
        pltpu.make_async_copy(value.at[:, own], value_own, sems.at[4]),
    ]
    for copy in copies:
        copy.start()
    for copy in copies[:3]:
        copy.wait()
    element(docs_held, key_held, value_held, out, 0, half)
    for copy in copies[3:]:
        copy.wait()


def second_kernel(docs, key, value, out, *, half):
    element(docs, key, value, out, 0, half)


def intra_kernel(docs, query, key, value, grad, own, message, *, half):
    both = one_doc(docs)
    tokens = query.shape[0]
    for other in (True, False):
        base = (1 - my_core() if other else my_core()) * half
        for heads in batches(half, 2):
            results = []
            for head in heads:
                full = wide(base, head)
                q = query[:, full]
                scores = lower(dot(q, key[:, full], 1, 1), both)
                part = times_lower(scores, value[:, full])
                results.append((q.astype(F32), grad[:, full].astype(F32), part) if other else (part,))
            for head, parts in zip(heads, results):
                cols = pl.ds(head * 128, 128)
                if other:
                    for at, part in enumerate(parts):
                        message[pl.ds(at * tokens, tokens), cols] = part
                else:
                    own[:, cols] = parts[0]


def attend(q, g, intra, state, gain, joined):
    inter = dot(q, state, 1, 0)
    attended = intra + jnp.concatenate([inter[:BLK], inter[BLK:] * joined], 0)
    inv_rms = lax.rsqrt(jnp.mean(attended * attended, -1, keepdims=True) + EPSILON)
    scaled = g * gain
    normed = attended * inv_rms
    terms = jnp.sum(g * normed, 0, keepdims=True)
    mean = jnp.mean(scaled * normed, -1, keepdims=True)
    attn = (inv_rms * (scaled - normed * mean)).astype(BF16)
    back = dot(q[:BLK], attn[:BLK], 0, 0) + dot(q[BLK:], attn[BLK:], 0, 0) * joined
    return attn, back, terms


def middle_kernel(
    docs, own, other, c0, c1, c2, c3, query, grad, intra, message, gain,
    up0, up1, up2, up3, back_own, back_other, attn_own, reply, state_own, *, half, size,
):
    rows, tokens, chunk = half * 128, query.shape[0], size // 128
    base = my_core() * half
    is_first = my_core() == 0
    own_first, own_last = row(own, rows, FIRST), row(own, rows, LAST)
    other_first, other_last = row(other, rows, FIRST), row(other, rows, LAST)
    keep_coming, keep_other, send_coming, send_own = spread_weights(
        is_first, own_first, own_last, other_first, other_last
    )
    own_joined, other_joined = match(own_first, own_last), match(other_first, other_last)
    for back, first, last in ((back_own, own_first, own_last), (back_other, other_first, other_last)):
        back[pl.ds(rows, IDS), :] = jnp.zeros((IDS, 128), F32)
        back[pl.ds(rows + FIRST, 1), :] = -last
        back[pl.ds(rows + LAST, 1), :] = -first
    first = jnp.minimum(own_first, other_first)
    last = jnp.maximum(own_last, other_last)
    own_weight, other_weight = match(own_first, first), match(other_first, first)
    ups = (up0, up1, up2, up3)
    for up in ups:
        up[pl.ds(size, 2 * IDS), :] = jnp.zeros((2 * IDS, 128), F32)
        up[pl.ds(size + FIRST, 1), :] = -last
        up[pl.ds(size + LAST, 1), :] = -first
    for turn, chip in enumerate((c0, c1, c2, c3)):
        results = []
        for step in range(chunk):
            head = lax.bitwise_xor(my_chip(), turn) * chunk + step
            cols, full = wide(0, head), wide(base, head)
            coming = chip[pl.ds(step * 128, 128), :]
            state = (coming * keep_coming + other[cols, :] * keep_other).astype(BF16)
            state_other = coming * send_coming + own[cols, :] * send_own
            weights = gain[pl.ds(base + head, 1), :]
            near = attend(
                query[:, full], grad[:, full].astype(F32), intra[:, cols], state, weights, own_joined
            )
            far = attend(
                message[pl.ds(0, tokens), cols].astype(BF16),
                message[pl.ds(tokens, tokens), cols],
                message[pl.ds(2 * tokens, tokens), cols],
                state_other.astype(BF16),
                weights,
                other_joined,
            )
            results.append((head, cols, state, state_other, near, far))
        for step, (head, cols, state, state_other, near, far) in enumerate(results):
            attn, back, terms = near
            attn_far, back_far, terms_far = far
            state_own[cols, :] = state
            reply[pl.ds(tokens, 128), cols] = state_other
            attn_own[:, cols] = attn
            back_own[cols, :] = back
            reply[pl.ds(0, tokens), cols] = attn_far.astype(F32)
            back_other[cols, :] = back_far
            ups[turn][pl.ds(step * 128, 128), :] = back * own_weight + back_far * other_weight
            for up in ups:
                up[pl.ds(size + IDS + head, 1), :] = terms + terms_far


def within_kernel(docs, query, key, value, *refs, half, other):
    query_grad, key_part, value_part, held, sems = refs[-5:]
    tokens = query.shape[0]
    both = one_doc(docs)
    enter32 = column(docs, True, F32)
    base = (1 - my_core() if other else my_core()) * half
    copies = []
    for heads in batches(half, 2):
        results = []
        for head in heads:
            cols, full = pl.ds(head * 128, 128), wide(base, head)
            q, k, v = query[:, full], key[:, full], value[:, full]
            if other:
                a = refs[0][pl.ds(0, tokens), cols].astype(BF16)
                state = refs[0][pl.ds(tokens, 128), cols].astype(BF16)
            else:
                a, state = refs[0][:, cols], refs[1][cols, :]
            pair = lower(dot(a, v, 1, 1), both)
            cross = enter32 * dot(a, state, 1, 1)
            results.append(
                (
                    (cross + times_lower(pair, k)).astype(BF16),
                    times_higher(higher(dot(v, a, 1, 1), both), q),
                    times_higher(higher(dot(k, q, 1, 1), both), a),
                )
            )
        for head, (query_part, key_term, value_term) in zip(heads, results):
            cols, full = pl.ds(head * 128, 128), wide(base, head)
            held[:, cols] = query_part
            copies.append(pltpu.make_async_copy(held.at[:, cols], query_grad.at[:, full], sems.at[head]))
            copies[-1].start()
            key_part[:, cols] = key_term
            value_part[:, cols] = value_term
    for copy in copies:
        copy.wait()


def finish_kernel(docs, key, value, key_part, value_part, state, *refs, half, other):
    refs, (key_held, value_held, gain_held, sems) = refs[:-4], refs[-4:]
    copies = []
    if other:
        refs, gain_grad = refs[:-1], refs[-1]
        for head in range(half):
            gain_held[pl.ds(my_core() * half + head, 1), :] = refs[0][pl.ds(head, 1), :]
            gain_held[pl.ds((1 - my_core()) * half + head, 1), :] = state[pl.ds(half * 128 + head, 1), :]
        copies.append(pltpu.make_async_copy(gain_held, gain_grad, sems.at[2, 0]))
        copies[-1].start()
    key_grad, value_grad = refs[-2:]
    leave = column(docs, False, F32)
    base = (1 - my_core() if other else my_core()) * half
    for at, heads in enumerate(batches(half, 4)):
        for head in heads:
            cols, full = pl.ds(head * 128, 128), wide(base, head)
            g = state[cols, :].astype(BF16)
            key_held[:, cols] = (key_part[:, cols] + leave * dot(value[:, full], g, 1, 1)).astype(BF16)
            value_held[:, cols] = (value_part[:, cols] + leave * dot(key[:, full], g, 1, 0)).astype(BF16)
        size = len(heads) * 128
        held = pl.ds(heads[0] * 128, size)
        full = pl.ds(pl.multiple_of((base + heads[0]) * 128, 128), size)
        copies.append(pltpu.make_async_copy(key_held.at[:, held], key_grad.at[:, full], sems.at[0, at]))
        copies.append(pltpu.make_async_copy(value_held.at[:, held], value_grad.at[:, full], sems.at[1, at]))
        copies[-2].start()
        copies[-1].start()
    for copy in copies:
        copy.wait()


def row(ref, rows, which):
    return ref[pl.ds(rows + which, 1), :]


def match(left, right):
    return jnp.where(left == right, 1.0, 0.0)


def pair_kernel(docs, own, other, *outs, half, size):
    rows = half * 128
    first = jnp.minimum(row(own, rows, FIRST), row(other, rows, FIRST))
    last = jnp.maximum(row(own, rows, LAST), row(other, rows, LAST))
    own_weight = match(row(own, rows, LAST), last)
    other_weight = match(row(other, rows, LAST), last)
    for turn, out in enumerate(outs):
        owner = lax.bitwise_xor(my_chip(), turn)
        part = pl.ds(pl.multiple_of(owner * size, size), size)
        out[pl.ds(0, size), :] = own[part, :] * own_weight + other[part, :] * other_weight
        out[pl.ds(size, IDS), :] = jnp.zeros((IDS, 128), F32)
        out[pl.ds(size + FIRST, 1), :] = first
        out[pl.ds(size + LAST, 1), :] = last


def plane_kernel(docs, c0, c1, c2, c3, out, *gain, size):
    chips = (c0, c1, c2, c3)
    last = functools.reduce(jnp.maximum, [row(c, size, LAST) for c in chips])
    out[pl.ds(0, size), :] = sum(
        c[pl.ds(0, size), :] * match(row(c, size, LAST), last) for c in chips
    )
    out[pl.ds(size, IDS), :] = jnp.zeros((IDS, 128), F32)
    out[pl.ds(size + LAST, 1), :] = last
    if gain:
        gain[0][...] = sum(c[pl.ds(size + IDS, IDS), :] for c in chips)
        out[pl.ds(size + IDS, IDS), :] = gain[0][...]


def chain_kernel(docs, c0, c1, c2, c3, *refs, size, distances, planes):
    chips = (c0, c1, c2, c3)
    backward = distances[0] < 0
    others, outs = refs[: len(distances)], refs[-CHIPS:]
    place = [lax.bitwise_xor(my_chip(), turn) for turn in range(CHIPS)]
    my_plane = lax.axis_index("ctx") // GROUP
    first = functools.reduce(jnp.minimum, [row(c, size, FIRST) for c in chips])
    coming = jnp.zeros((size, 128), F32)
    for distance, other in zip(distances, others):
        source = my_plane - distance
        inside = (source >= 0) & (source < planes)
        weight = match(row(other, size, LAST), first) * jnp.where(inside, 1.0, 0.0)
        coming = coming + other[pl.ds(0, size), :] * weight
    if backward:
        gain, sums, outs = refs[len(distances)], refs[-1], refs[-1 - CHIPS : -1]
        sums[...] = gain[...] + sum(p[pl.ds(size + IDS, IDS), :] for p in others)
    for turn, out in enumerate(outs):
        mine = row(chips[turn], size, FIRST)
        total = coming * match(mine, first)
        for other in range(CHIPS):
            if other == turn:
                continue
            ahead = place[other] > place[turn] if backward else place[other] < place[turn]
            weight = match(row(chips[other], size, LAST), mine) * jnp.where(ahead, 1.0, 0.0)
            total = total + chips[other][pl.ds(0, size), :] * weight
        out[...] = total


def spread_weights(is_first, own_first, own_last, other_first, other_last):
    ones = jnp.ones((1, 128), F32)
    joins = match(own_first, other_first)
    return (
        jnp.where(is_first, ones, joins),
        jnp.where(is_first, 0.0 * ones, match(other_last, own_first)),
        jnp.where(is_first, joins, ones),
        jnp.where(is_first, match(own_last, other_first), 0.0 * ones),
    )


def spread_kernel(docs, own, other, c0, c1, c2, c3, sums, sums_near, send, keep, total, *, half, size):
    rows = half * 128
    keep_coming, keep_other, send_coming, send_own = spread_weights(
        my_core() == 1,
        row(own, rows, FIRST),
        row(own, rows, LAST),
        row(other, rows, FIRST),
        row(other, rows, LAST),
    )
    for turn, chip in enumerate((c0, c1, c2, c3)):
        owner = lax.bitwise_xor(my_chip(), turn)
        part = pl.ds(pl.multiple_of(owner * size, size), size)
        coming = chip[pl.ds(0, size), :]
        send[part, :] = coming * send_coming + own[part, :] * send_own
        keep[part, :] = (coming * keep_coming + other[part, :] * keep_other).astype(BF16)
    total[...] = sums[...] + sums_near[...]
    send[pl.ds(rows, IDS), :] = total[...]


def shape(rows, cols, dtype):
    return jax.ShapeDtypeStruct((rows, cols), dtype)


def call(kernel, docs, args, outs, flops=0, in_specs=None, out_specs=None, aliases=None, scratch=()):
    whole = pl.BlockSpec(memory_space=pltpu.VMEM)
    in_specs = in_specs or [None] * len(args)
    out_specs = out_specs or [None] * len(outs)
    moved = sum(a.size * a.dtype.itemsize for a in list(args) + list(outs))
    return pl.pallas_call(
        kernel,
        out_shape=outs,
        grid_spec=pltpu.PrefetchScalarGridSpec(
            num_scalar_prefetch=1,
            grid=(1,),
            in_specs=[spec or whole for spec in in_specs],
            out_specs=[spec or whole for spec in out_specs],
            scratch_shapes=scratch,
        ),
        input_output_aliases=aliases or {},
        cost_estimate=pl.CostEstimate(flops=flops, bytes_accessed=moved, transcendentals=0),
        compiler_params=pltpu.CompilerParams(vmem_limit_bytes=32 * 1024 * 1024),
    )(docs, *args)


def tie(value, *after):
    return lax.optimization_barrier((value, after))[0]


def local(queries, key_rows, value_rows, out_grad, norm_gain, doc_ids, *, shards, dp):
    tokens = queries.shape[1]
    heads, width = norm_gain.shape
    half = heads // 2
    rows, cols = half * width, heads * width
    size = rows // CHIPS
    query, key, value, grad = (
        a.reshape(tokens, cols) for a in (queries, key_rows, value_rows, out_grad)
    )
    planes = shards // GROUP
    any_place = pl.BlockSpec(memory_space=pl.ANY)

    def swap(value):
        return lax.ppermute(value, "ctx", [(i, i ^ 1) for i in range(shards)])

    def to_chips(values):
        return [values[0]] + [
            lax.ppermute(values[turn], "ctx", [(i, i ^ (2 * turn)) for i in range(shards)])
            for turn in (1, 2, 3)
        ]

    def around(value, distance):
        pairs = [(i, (i + distance * GROUP) % shards) for i in range(shards)]
        return lax.ppermute(value, "ctx", pairs)

    payload = shape(rows + IDS, width, F32)

    def chain(sent, backward, beside_up, beside_planes, beside_down):
        chunks = tie(to_chips(sent), beside_up(sent))
        plane, *gain = call(
            functools.partial(plane_kernel, size=size),
            doc_ids,
            chunks,
            [shape(size + (2 * IDS if backward else IDS), width, F32)]
            + ([shape(IDS, width, F32)] if backward else []),
        )
        distances = (-1, -2) if backward else (1, 2)
        others = [around(plane, distance) for distance in distances]
        others = tie(others, beside_planes(plane, others))
        sent = call(
            functools.partial(chain_kernel, size=size, distances=distances, planes=planes),
            doc_ids,
            [*chunks, *others, *gain],
            [shape(size, width, F32)] * CHIPS + ([shape(IDS, width, F32)] if backward else []),
        )
        return tie(to_chips(sent[:CHIPS]), beside_down(sent, *gain))

    def within(other, sources, into):
        spare = [] if into is None else [into]
        at = 3 + len(sources)
        return call(
            functools.partial(within_kernel, half=half, other=other),
            doc_ids,
            [query, key, value, *sources, *spare],
            [shape(tokens, cols, BF16), shape(tokens, rows, F32), shape(tokens, rows, F32)],
            flops=2 * half * tokens * width * (6 * tokens + width),
            in_specs=[None] * at + [any_place] * len(spare),
            out_specs=[any_place] + [None] * 2,
            aliases={1 + at: 0} if spare else None,
            scratch=[pltpu.VMEM((tokens, rows), BF16), pltpu.SemaphoreType.DMA((half,))],
        )

    def finish(other, parts, state, sums, into):
        return call(
            functools.partial(finish_kernel, half=half, other=other),
            doc_ids,
            [key, value, *parts, state, *sums, *into],
            [shape(tokens, cols, BF16)] * 2 + [shape(heads, width, F32)] * len(sums),
            flops=2 * half * tokens * width * 2 * width,
            in_specs=[None] * (5 + len(sums)) + [any_place] * len(into),
            out_specs=[any_place] * (2 + len(sums)),
            aliases={7: 0, 8: 1} if into else None,
            scratch=[
                pltpu.VMEM((tokens, rows), BF16),
                pltpu.VMEM((tokens, rows), BF16),
                pltpu.VMEM((heads, width), F32),
                pltpu.SemaphoreType.DMA((3, half)),
            ],
        )

    hbm = pl.BlockSpec(memory_space=pltpu.HBM)
    vmem = pl.BlockSpec(memory_space=pltpu.VMEM)
    half_shape = shape(tokens, rows, BF16)
    states, key_own, value_own = pl.pallas_call(
        functools.partial(first_kernel, half=half),
        out_shape=[payload, half_shape, half_shape],
        in_specs=[hbm] * 3,
        out_specs=[vmem] * 3,
        scratch_shapes=[
            pltpu.SMEM(doc_ids.shape, jnp.int32),
            pltpu.VMEM(half_shape.shape, BF16),
            pltpu.VMEM(half_shape.shape, BF16),
            pltpu.SemaphoreType.DMA((5,)),
        ],
        cost_estimate=pl.CostEstimate(
            flops=2 * half * tokens * width * width, bytes_accessed=4 * tokens * rows * 2, transcendentals=0
        ),
        compiler_params=pltpu.CompilerParams(vmem_limit_bytes=32 * 1024 * 1024),
    )(*(pltpu.with_memory_space_constraint(x, pltpu.HBM) for x in (doc_ids, key, value)))
    received = swap(states)
    query, key, value, grad, doc_ids = tie((query, key, value, grad, doc_ids), states)
    (own,) = call(
        functools.partial(second_kernel, half=half),
        doc_ids,
        [key_own, value_own],
        [payload],
        flops=2 * half * tokens * width * width,
    )
    sent = call(
        functools.partial(pair_kernel, half=half, size=size),
        doc_ids,
        [own, received],
        [shape(size + IDS, width, F32)] * CHIPS,
    )

    kept = {}

    def intra(sent):
        kept["inside"], kept["message"] = call(
            functools.partial(intra_kernel, half=half),
            doc_ids,
            [tie(query, sent), key, value, grad],
            [shape(tokens, rows, F32), shape(3 * tokens, rows, F32)],
            flops=2 * heads * tokens * width * 2 * tokens,
        )
        return kept["inside"]

    def forward_message(plane, others):
        kept["message"] = swap(tie(kept["message"], plane))
        return []

    coming = chain(sent, False, intra, forward_message, lambda sent: [])
    *sent, back, back_other, attn, reply, state = call(
        functools.partial(middle_kernel, half=half, size=size),
        doc_ids,
        [own, received, *coming, query, grad, kept["inside"], kept["message"], norm_gain],
        [shape(size + 2 * IDS, width, F32)] * CHIPS
        + [payload, payload]
        + [shape(tokens, rows, BF16), shape(tokens + width, rows, F32), shape(rows, width, BF16)],
        flops=2 * heads * tokens * width * 2 * width,
    )

    def beside_up(sent):
        kept["first"] = within(False, [tie(attn, sent), state], None)
        return kept["first"]

    def beside_planes(plane, others):
        kept["reply"] = swap(tie(reply, others))
        return []

    def beside_down(sent, gain):
        kept["sums"] = [sent[-1], around(tie(gain, sent), 1)]
        kept["second"] = within(True, [tie(kept["reply"], sent)], kept["first"][0])
        return kept["second"]

    coming = chain(sent, True, beside_up, beside_planes, beside_down)
    send, out_state, total = call(
        functools.partial(spread_kernel, half=half, size=size),
        doc_ids,
        [back, back_other, *coming, *kept["sums"]],
        [shape(rows + IDS, width, F32), shape(rows, width, BF16), shape(IDS, width, F32)],
    )
    out_received = swap(send)
    grads = finish(False, kept["first"][1:], out_state, [], [])
    out_received, grads = lax.optimization_barrier((out_received, grads))
    query_grad, *parts = kept["second"]
    key_grad, value_grad, gain_grad = finish(True, parts, out_received, [total], grads)
    if dp > 1:
        gain_grad = lax.psum_scatter(gain_grad, "dp", scatter_dimension=1, tiled=True)
    flat = (1, tokens, cols)
    return (query_grad.reshape(flat), key_grad.reshape(flat), value_grad.reshape(flat), gain_grad)


def solution(mesh):
    in_specs = (
        P("dp", "ctx", "tp"),
        P("dp", "ctx", "tp"),
        P("dp", "ctx", "tp"),
        P("dp", "ctx", "tp"),
        P("tp", None),
        P("dp", "ctx"),
    )
    out_specs = (P("dp", "ctx", "tp"), P("dp", "ctx", "tp"), P("dp", "ctx", "tp"), P("tp", "dp"))
    body = functools.partial(local, shards=mesh.shape["ctx"], dp=mesh.shape["dp"])
    return jax.shard_map(body, mesh=mesh, in_specs=in_specs, out_specs=out_specs, check_vma=False)
```
